256 devices in a mesh: pts: 32 (over x, z), cent: 8 (over y, core).
Axes of the slice: x: 4, y: 4, z: 8, core: 2. Of those that a mesh axis runs over, the one named last changes fastest.
Arguments:
- points: bfloat16 [16384, 1024], P('pts'), may hold values from -20 to 20
- centroids: bfloat16 [25600, 1024], P('cent'), may hold values from -0.7 to 0.7
Outputs:
- level_four_points: bfloat16 [25600, 1024], P('pts', 'cent')
The draws below stay inside these ranges and needn't reach their ends.
All inputs are finite; a program needn't handle non-finite values.
Results may differ from the reference program's by a relative error of at most 0.0059.
Values may be sent and summed in bfloat16 or wider, within the bound.
No kernel may reach another device: no remote copies, remote signals or barrier semaphores. Data moves between devices by JAX's collectives and lax.ppermute only.
A program may use at most 64 MiB of HBM per device.

```python
import math
import jax
import jax.numpy as jnp
from jax import lax

D = 1024
K = 25600
POINTS = 16384
N_PTS = 32
N_CENT = 8


def drawn_pairs(key):
    pair_count = POINTS // 64
    shuffled = jax.random.permutation(jax.random.fold_in(key, 21), K // 2)
    pair_rows = 2 * shuffled[:pair_count].astype(jnp.int32)
    levels = jnp.array([8.0, 15.0, 22.0], jnp.float32)
    strength = levels[jnp.arange(pair_count) % 3]
    return (pair_rows, strength)


def centroid_table(key):
    raw_table = 0.1 * jnp.clip(jax.random.normal(jax.random.fold_in(key, 31), (K, D), jnp.float32), -6.0, 6.0)
    pair_rows, strength = drawn_pairs(key)
    target_norm = 16.0
    amplitude = jnp.sqrt(target_norm / D)
    planted = amplitude * jnp.where(raw_table[pair_rows] >= 0.0, 1.0, -1.0)
    stretch = 2.0 / ((strength - 1.0) * target_norm)
    partner = planted * (1.0 + stretch)[:, None]
    return raw_table.at[pair_rows].set(planted).at[pair_rows + 1].set(partner)


def draw_centroids(key, part):
    return centroid_table(key).astype(jnp.bfloat16)


def planted_points(key, base_rows):
    centroid_rows = centroid_table(key).astype(jnp.bfloat16).astype(jnp.float32)
    pair_rows, strength = drawn_pairs(key)
    slot_index = 5 + 64 * jnp.arange(POINTS // 64)
    return base_rows.at[slot_index].set(strength[:, None] * centroid_rows[pair_rows])


def draw_points(key, part):
    inner = jax.random.fold_in(key, 5)
    base_rows = jnp.clip(jax.random.normal(inner, (POINTS, D), jnp.float32), -6.0, 6.0)
    return planted_points(key, base_rows).astype(jnp.bfloat16)


def setup_inputs(seed: int = 0) -> dict:
    seeds = jax.random.split(jax.random.key(seed), 3)
    points = draw_points(jax.random.fold_in(seeds[2], 71), 0)
    centroids = draw_centroids(jax.random.fold_in(seeds[2], 71), 0)
    return dict(points=points, centroids=centroids)


def regroup_rows(updated):
    slot_rows = K // (N_PTS * N_CENT)
    return updated.reshape(N_CENT, N_PTS, slot_rows, D).transpose(1, 0, 2, 3).reshape(K, D)


def reference(points, centroids):
    half_norms = 0.5 * jnp.sum(jnp.square(centroids.astype(jnp.float32)), axis=1)
    block_size = math.gcd(POINTS, 1024)
    blocks = points.reshape(POINTS // block_size, block_size, D)

    def accumulate(state_pair, block_rows):
        logits = jnp.dot(block_rows, centroids.T, preferred_element_type=jnp.float32) - half_norms[None, :]
        row_top = jnp.max(logits, axis=1, keepdims=True)
        exponent = jnp.exp(logits - row_top)
        weights = (exponent / jnp.sum(exponent, axis=1, keepdims=True)).astype(jnp.bfloat16)
        numerator = state_pair[0] + jnp.dot(weights.T, block_rows, preferred_element_type=jnp.float32)
        counts = state_pair[1] + jnp.sum(weights.astype(jnp.float32), axis=0)
        return (numerator, counts), None

    initial = (jnp.zeros((K, D), jnp.float32), jnp.zeros((K,), jnp.float32))
    (numerator, counts), unused = lax.scan(accumulate, initial, blocks)
    updated = numerator / (counts[:, None] + 1.0)
    return regroup_rows(updated).astype(jnp.bfloat16)
```

```python
import jax
import jax.numpy as jnp
from jax import lax
from jax.sharding import Mesh, PartitionSpec as P

BF = jnp.bfloat16
F32 = jnp.float32


def dot_nt(a, b):
    return lax.dot_general(a, b, (((1,), (1,)), ((), ())), preferred_element_type=F32)


def share(a, axes, n):
    return lax.all_to_all(jnp.broadcast_to(a[None], (n, *a.shape)), axes, 0, 0)


def body(points, centroids):
    n_x, n_z, n_y, n_core = (lax.axis_size(a) for a in ("x", "z", "y", "core"))
    n_cent = n_y * n_core
    rows, dim = centroids.shape
    pts = points.shape[0]
    slot = rows // (n_x * n_z)
    cols = dim // n_cent
    me_z, me_core = lax.axis_index("z"), lax.axis_index("core")

    half = lax.dynamic_slice_in_dim(points, me_core * (pts // n_core), pts // n_core, 0)
    gathered = lax.all_gather(half, ("z", "core"), tiled=True)

    half_norms = 0.5 * jnp.sum(jnp.square(centroids.astype(F32)), axis=1)
    logits = dot_nt(points, centroids) - half_norms[None, :]
    top = jnp.max(logits, axis=1)
    total = jnp.sum(jnp.exp(logits - top[:, None]), axis=1)
    stats = share(jnp.stack([top, total]), ("y", "core"), n_cent)
    row_top = jnp.max(stats[:, 0], axis=0)
    lse = row_top + jnp.log(jnp.sum(stats[:, 1] * jnp.exp(stats[:, 0] - row_top[None]), axis=0))
    all_lse = share(lse, "z", n_z).reshape(-1)

    mine = lax.dynamic_index_in_dim(centroids.reshape(n_x, n_z, slot, dim), me_z, 1, keepdims=False)
    mine = mine.reshape(n_x * slot, dim)
    norms = lax.dynamic_index_in_dim(half_norms.reshape(n_x, n_z, slot), me_z, 1, keepdims=False).reshape(-1)

    logits2 = dot_nt(gathered, mine) - norms[None, :] - all_lse[:, None]
    weights = jnp.exp(logits2).astype(BF)
    counts = jnp.sum(weights.astype(F32), axis=0).reshape(n_x, 1, 1, slot)
    numer = lax.dot_general(weights, gathered, (((0,), (0,)), ((), ())), preferred_element_type=F32)
    numer = numer.astype(BF).reshape(n_x, slot, n_cent, cols).transpose(0, 2, 1, 3)
    high = counts.astype(BF)
    low = (counts - high.astype(F32)).astype(BF)
    tail = jnp.concatenate([high, low], axis=2)
    tail = jnp.pad(tail, ((0, 0), (0, 0), (0, 2), (0, cols - slot)))
    tail = jnp.broadcast_to(tail, (n_x, n_cent, 4, cols))
    send = jnp.concatenate([numer, tail], axis=2).reshape(n_x * n_cent, slot + 4, cols)
    got = lax.all_to_all(send, ("x", "y", "core"), 0, 0)
    got = jnp.sum(got.reshape(n_x, n_cent, slot + 4, cols).astype(F32), axis=0)
    count = got[:, slot, :slot] + got[:, slot + 1, :slot]
    out = got[:, :slot] / (count[:, :, None] + 1.0)
    return out.astype(BF).reshape(n_cent * slot, cols)


def solution(mesh):
    fine = Mesh(mesh.devices.reshape(4, 8, 4, 2), ("x", "z", "y", "core"))
    pts, cent = ("x", "z"), ("y", "core")
    return jax.shard_map(
        body, mesh=fine, in_specs=(P(pts, None), P(cent, None)), out_specs=P(pts, cent), check_vma=False
    )
```

```python
import jax
import jax.numpy as jnp
from jax import lax
from jax.sharding import Mesh, PartitionSpec as P

BF = jnp.bfloat16
F32 = jnp.float32
NX, NZ, NY, NC = 4, 8, 4, 2
Z = ("zq", "zp")
CENT = ("y", "core")
TAIL = 4


def dot_nt(a, b):
    return lax.dot_general(a, b, (((1,), (1,)), ((), ())), preferred_element_type=F32)


def share(a, axes, n):
    return lax.all_to_all(jnp.broadcast_to(a[None], (n, *a.shape)), axes, 0, 0)


def split(counts):
    high = counts.astype(BF)
    return high, (counts - high.astype(F32)).astype(BF)


def body(points, centroids):
    rows, dim = centroids.shape
    pts = points.shape[0]
    n_cent = NY * NC
    slot = rows // (NX * NZ)
    cols = dim // n_cent
    mine = rows // NX
    half = pts // NC
    x, parity, core = lax.axis_index("x"), lax.axis_index("zp"), lax.axis_index("core")

    own = lax.dynamic_slice_in_dim(points, core * half, half, 0)
    shards = {
        k: lax.ppermute(own, "x", [(i, (i + k) % NX) for i in range(NX)]) for k in (1, 3, 2)
    }
    other = {k: lax.ppermute(a, "core", [(0, 1), (1, 0)]) for k, a in shards.items()}

    half_norms = 0.5 * jnp.sum(jnp.square(centroids.astype(F32)), axis=1)
    logits = dot_nt(points, centroids) - half_norms[None, :]
    top = jnp.max(logits, axis=1)
    total = jnp.sum(jnp.exp(logits - top[:, None]), axis=1)
    stats = share(jnp.stack([top, total]), ("x", *CENT), NX * n_cent)
    stats = stats.reshape(NX, n_cent, 2, pts)
    row_top = jnp.max(stats[:, :, 0], axis=1)
    row_sum = jnp.sum(stats[:, :, 1] * jnp.exp(stats[:, :, 0] - row_top[:, None]), axis=1)
    lse = row_top + jnp.log(row_sum)

    blocks = lax.dynamic_slice_in_dim(centroids, x * mine, mine, 0).reshape(NZ // 2, 2, slot, dim)
    norms = lax.dynamic_slice_in_dim(half_norms, x * mine, mine, 0).reshape(NZ // 2, 2, slot)
    pad = ((0, 0), (0, TAIL), (0, 0))

    def pick(p):
        rows_p = jnp.pad(lax.dynamic_index_in_dim(blocks, p, 1, keepdims=False), pad)
        norms_p = jnp.pad(lax.dynamic_index_in_dim(norms, p, 1, keepdims=False), pad[:2])
        return rows_p.reshape(-1, dim), norms_p.reshape(-1)

    all_points = [points]
    all_lse = [lax.dynamic_index_in_dim(lse, x, 0, keepdims=False)]
    for k in (1, 3, 2):
        source = lax.dynamic_index_in_dim(lse, lax.rem(x + NX - k, NX), 0, keepdims=False)
        all_points += [shards[k], other[k]]
        all_lse += [
            lax.dynamic_slice_in_dim(source, core * half, half, 0),
            lax.dynamic_slice_in_dim(source, (1 - core) * half, half, 0),
        ]
    all_points = jnp.concatenate(all_points, axis=0)
    all_lse = jnp.concatenate(all_lse, axis=0)

    def partial(p):
        rows_p, norms_p = pick(p)
        weights = jnp.exp(dot_nt(rows_p, all_points) - norms_p[:, None] - all_lse[None, :]).astype(BF)
        counts = jnp.sum(weights.astype(F32), axis=1).reshape(NZ // 2, slot + TAIL)
        numer = jnp.dot(weights, all_points, preferred_element_type=F32)
        return numer.reshape(NZ // 2, slot + TAIL, dim), counts

    def tails(counts):
        high, low = split(counts)
        tail = jnp.stack([high[..., :slot], low[..., :slot]], axis=1)
        return jnp.pad(tail, ((0, 0), (0, TAIL - 2), (0, cols - slot)))

    def counts_of(a):
        return a[:, slot, :slot].astype(F32) + a[:, slot + 1, :slot].astype(F32)

    give, give_counts = partial(1 - parity)
    tail = jnp.tile(tails(give_counts), (1, 1, n_cent // 2))
    given = []
    for h in range(2):
        part = give[:, :slot, h * dim // 2 : (h + 1) * dim // 2].astype(BF)
        part = jnp.concatenate([part, tail], axis=1)
        pairs = [(i, i ^ 1) for i in range(NZ)] if h == 0 else [(i, (i + (1 if i % 2 else -1)) % NZ) for i in range(NZ)]
        given.append(lax.ppermute(part, Z, pairs))
    keep, keep_counts = partial(parity)
    merged = []
    for h in range(2):
        part = keep[:, :slot, h * dim // 2 : (h + 1) * dim // 2] + given[h][:, :slot].astype(F32)
        tail = jnp.tile(tails(keep_counts[:, :slot] + counts_of(given[h])), (1, 1, n_cent // 2))
        merged.append(jnp.concatenate([part.astype(BF), tail], axis=1))
    merged = jnp.concatenate(merged, axis=2)
    send = merged.reshape(NZ // 2, slot + TAIL, n_cent, cols).transpose(0, 2, 1, 3)
    got = lax.all_to_all(send.reshape(-1, slot + TAIL, cols), ("zq", *CENT), 0, 0)
    got = jnp.sum(got.reshape(NZ // 2, n_cent, slot + TAIL, cols).astype(F32), axis=0)
    out = got[:, :slot] / (counts_of(got)[:, :, None] + 1.0)
    return out.astype(BF).reshape(n_cent * slot, cols)


def solution(mesh):
    fine = Mesh(mesh.devices.reshape(NX, NZ // 2, 2, NY, NC), ("x", *Z, *CENT))
    pts = ("x", *Z)
    return jax.shard_map(
        body, mesh=fine, in_specs=(P(pts, None), P(CENT, None)), out_specs=P(pts, CENT), check_vma=False
    )
```

```python
import functools

import jax
import jax.numpy as jnp
from jax import lax
from jax.experimental import pallas as pl
from jax.experimental.pallas import tpu as pltpu
from jax.sharding import Mesh, PartitionSpec as P

BF = jnp.bfloat16
F32 = jnp.float32
NX, NZ, NY, NC = 4, 8, 4, 2
Z = ("zq", "zp")
CENT = ("y", "core")
N_CENT = NY * NC
LANES = 128
TAIL = 4
VMEM = pl.BlockSpec(memory_space=pltpu.VMEM)
SMEM = pl.BlockSpec(memory_space=pltpu.SMEM)
ANY = pl.BlockSpec(memory_space=pl.ANY)
LIMIT = 40 * 2**20


def dot_nt(a, b):
    return lax.dot_general(a, b, (((1,), (1,)), ((), ())), preferred_element_type=F32)


def params():
    return pltpu.CompilerParams(vmem_limit_bytes=LIMIT)


def cost(flops, read):
    return pl.CostEstimate(flops=flops, bytes_accessed=read, transcendentals=0)


def cut_kernel(place, points, half_out, eighth_out, sem):
    half, eighth = half_out.shape[0], eighth_out.shape[0]
    a = pltpu.make_async_copy(points.at[pl.ds(pl.multiple_of(place[0] * half, half), half)], half_out, sem.at[0])
    b = pltpu.make_async_copy(
        points.at[pl.ds(pl.multiple_of(place[1] * eighth, eighth), eighth)], eighth_out, sem.at[1]
    )
    a.start()
    b.start()
    a.wait()
    b.wait()


def stats_kernel(points, cents, out, top, total):
    step = pl.program_id(0)
    rows = cents[...]
    wide = rows.astype(F32)
    norms = 0.5 * jnp.sum(wide * wide, axis=1, keepdims=True)
    logits = dot_nt(rows, points[...]) - norms
    tile_top = jnp.max(logits, axis=0, keepdims=True)

    @pl.when(step == 0)
    def _():
        top[...] = tile_top
        total[...] = jnp.zeros_like(total)

    old = top[...]
    new = jnp.maximum(old, tile_top)
    total[...] = total[...] * jnp.exp(old - new) + jnp.sum(jnp.exp(logits - new), axis=0, keepdims=True)
    top[...] = new

    @pl.when(step == pl.num_programs(0) - 1)
    def _():
        groups = top.shape[1] // LANES
        tile = jnp.concatenate(
            [r[:, g * LANES : (g + 1) * LANES] for r in (top[...], total[...]) for g in range(groups)], axis=0
        )
        out[...] = jnp.broadcast_to(tile[None], out.shape)


def weighted(place, stats, own, near, cents, norms, weights):
    x, core = place[2], place[0]
    groups = stats.shape[1] // 2

    def lse_of(source):
        part = stats[pl.ds(source * N_CENT, N_CENT)]
        m, s = part[:, :groups], part[:, groups:]
        high = jnp.max(m, axis=0)
        return high + jnp.log(jnp.sum(s * jnp.exp(m - high[None]), axis=0))

    pieces = []
    lse = lse_of(x)
    pieces.append((own, [lse[g : g + 1] for g in range(groups)]))
    for k, mine, other in near:
        lse = lse_of(lax.rem(x + NX - k, NX))
        low, high = lse[: groups // 2], lse[groups // 2 :]
        first = core == 0
        for ref, part in ((mine, jnp.where(first, low, high)), (other, jnp.where(first, high, low))):
            pieces.append((ref, [part[g : g + 1] for g in range(groups // 2)]))
    rows = cents[...]
    shift = norms[...]
    counts = jnp.zeros((rows.shape[0], LANES), F32)
    at = 0
    numer = None
    for ref, parts in pieces:
        block = ref[...]
        logits = dot_nt(rows, block)
        chunk = []
        for g, part in enumerate(parts):
            w = jnp.exp(logits[:, g * LANES : (g + 1) * LANES] - shift - part).astype(BF)
            counts += w.astype(F32)
            chunk.append(w)
        term = jnp.dot(jnp.concatenate(chunk, axis=1), block, preferred_element_type=F32)
        numer = term if numer is None else numer + term
    return numer, counts


def row_counts(counts, block, height):
    part = counts[block * height : (block + 1) * height]
    part = jnp.concatenate([part, jnp.zeros((LANES - height, LANES), F32)], axis=0)
    return jnp.sum(part.T, axis=0, keepdims=True)


def close(values, first, second):
    height, width = values.shape
    first = jnp.concatenate([first] * (width // LANES), axis=1)
    second = jnp.concatenate([second] * (width // LANES), axis=1)
    last = values[height - 8 :]
    row = lax.broadcasted_iota(jnp.int32, last.shape, 0)
    last = jnp.where(row == 8 - TAIL, first, jnp.where(row == 9 - TAIL, second, jnp.where(row > 9 - TAIL, 0.0, last)))
    return jnp.concatenate([values[: height - 8], last], axis=0)


def split(counts):
    high = counts.astype(BF).astype(F32)
    return high, counts - high


def give_kernel(place, stats, own, a1, a3, a2, b1, b3, b2, cents, norms, left, right, weights):
    numer, counts = weighted(place, stats, own, ((1, a1, b1), (3, a3, b3), (2, a2, b2)), cents, norms, weights)
    blocks, height, width = left.shape
    for b in range(blocks):
        high, low = split(row_counts(counts, b, height))
        values = close(numer[b * height : (b + 1) * height], high, low).astype(BF)
        left[b] = values[:, :width]
        right[b] = values[:, width:]


def keep_kernel(place, stats, own, a1, a3, a2, b1, b3, b2, cents, norms, kept, weights):
    numer, counts = weighted(place, stats, own, ((1, a1, b1), (3, a3, b3), (2, a2, b2)), cents, norms, weights)
    blocks, height, width = kept.shape
    for b in range(blocks):
        total = row_counts(counts, b, height)
        kept[b] = close(numer[b * height : (b + 1) * height], total, jnp.zeros_like(total))


def merge_kernel(kept, left, right, send):
    blocks, height, width = kept.shape
    at = height - TAIL
    for b in range(blocks):
        for h, got in ((0, left), (1, right)):
            half = width // 2
            mine = kept[b, :, h * half : (h + 1) * half]
            theirs = got[b].astype(F32)
            values = mine + theirs
            tail = values[height - 8 :]
            counts = tail[8 - TAIL : 9 - TAIL, :LANES] + tail[9 - TAIL : 10 - TAIL, :LANES]
            high, low = split(counts)
            values = close(values, high, low).astype(BF)
            for c in range(half // LANES):
                send[b * N_CENT + h * (half // LANES) + c] = values[:, c * LANES : (c + 1) * LANES]


def final_kernel(got, out, scratch):
    n, height, _ = got.shape
    slot = height - TAIL
    for c in range(N_CENT):
        values = got[c].astype(F32)
        for i in range(1, n // N_CENT):
            values += got[i * N_CENT + c].astype(F32)
        tail = values[height - 8 :]
        counts = tail[8 - TAIL : 9 - TAIL] + tail[9 - TAIL : 10 - TAIL] + 1.0
        column = jnp.broadcast_to(counts, (LANES, LANES)).T
        scratch[c * slot : (c + 1) * slot] = (values / column[:height])[:slot]
    out[...] = scratch[...].astype(BF)


def body(points, centroids):
    rows, dim = centroids.shape
    pts = points.shape[0]
    slot = rows // (NX * NZ)
    height = slot + TAIL
    mine = rows // NX
    half, eighth = pts // NC, pts // N_CENT
    x, y, parity, core = (lax.axis_index(a) for a in ("x", "y", "zp", "core"))
    place = jnp.stack([core, core * NY + y, x]).astype(jnp.int32)
    shape = jax.ShapeDtypeStruct

    own_half, own_eighth = pl.pallas_call(
        cut_kernel,
        out_shape=(shape((half, dim), BF), shape((eighth, dim), BF)),
        in_specs=[SMEM, ANY],
        out_specs=(VMEM, VMEM),
        scratch_shapes=[pltpu.SemaphoreType.DMA((2,))],
        compiler_params=params(),
        cost_estimate=cost(0, 2 * half * dim * 2),
        name="cut",
    )(place, points)

    def ring(a, k):
        return lax.ppermute(a, "x", [(i, (i + k) % NX) for i in range(NX)])

    far = ring(own_eighth, 2)
    shards = {1: ring(own_half, 1), 3: ring(own_half, 3)}

    tile = 640
    send_stats = pl.pallas_call(
        stats_kernel,
        grid=(rows // tile,),
        out_shape=shape((NX * N_CENT, 2 * pts // LANES, LANES), F32),
        in_specs=[pl.BlockSpec((pts, dim), lambda i: (0, 0)), pl.BlockSpec((tile, dim), lambda i: (i, 0))],
        out_specs=pl.BlockSpec((NX * N_CENT, 2 * pts // LANES, LANES), lambda i: (0, 0, 0)),
        scratch_shapes=[pltpu.VMEM((1, pts), F32), pltpu.VMEM((1, pts), F32)],
        compiler_params=params(),
        cost_estimate=cost(2 * pts * rows * dim, rows * dim * 2),
        name="stats",
    )(points, centroids)
    far, centroids, send_stats = lax.optimization_barrier((far, centroids, send_stats))
    stats = lax.all_to_all(send_stats, ("x", *CENT), 0, 0)

    slices = [far] + [lax.ppermute(far, "y", [(i, i ^ k) for i in range(NY)]) for k in range(1, NY)]
    order = jnp.stack(slices)
    shards[2] = jnp.concatenate([lax.dynamic_index_in_dim(order, y ^ k, 0, keepdims=False) for k in range(NY)], axis=0)
    shards, stats = lax.optimization_barrier((shards, stats))
    other = {k: lax.ppermute(a, "core", [(0, 1), (1, 0)]) for k, a in shards.items()}

    blocks = lax.dynamic_slice_in_dim(centroids, x * mine, mine, 0).reshape(NZ // 2, 2, slot, dim)

    def pick(p):
        part = jnp.pad(lax.dynamic_index_in_dim(blocks, p, 1, keepdims=False), ((0, 0), (0, TAIL), (0, 0)))
        part = part.reshape(-1, dim)
        return part, 0.5 * jnp.sum(jnp.square(part.astype(F32)), axis=1, keepdims=True)

    pieces = (points, shards[1], shards[3], shards[2], other[1], other[3], other[2])
    work = NZ // 2 * height
    total = NX * pts

    def call(kernel, p, out_shape):
        return pl.pallas_call(
            kernel,
            out_shape=out_shape,
            in_specs=[SMEM] + [VMEM] * 10,
            out_specs=jax.tree.map(lambda _: VMEM, out_shape),
            scratch_shapes=[pltpu.VMEM((8, LANES), BF)],
            compiler_params=params(),
            cost_estimate=cost(4 * work * total * dim, total * dim * 2),
            name=kernel.__name__,
        )(place, stats, *pieces, *pick(p))

    n_blocks = NZ // 2
    part = shape((n_blocks, height, dim // 2), BF)
    left, right = call(give_kernel, 1 - parity, (part, part))
    got_left = lax.ppermute(left, Z, [(i, i ^ 1) for i in range(NZ)])
    got_right = lax.ppermute(right, Z, [(i, (i + (1 if i % 2 else -1)) % NZ) for i in range(NZ)])
    kept = call(keep_kernel, parity, shape((n_blocks, height, dim), F32))
    send = pl.pallas_call(
        merge_kernel,
        out_shape=shape((n_blocks * N_CENT, height, LANES), BF),
        in_specs=[VMEM] * 3,
        out_specs=VMEM,
        compiler_params=params(),
        name="merge",
    )(kept, got_left, got_right)
    got = lax.all_to_all(send, ("zq", *CENT), 0, 0)
    return pl.pallas_call(
        final_kernel,
        out_shape=shape((N_CENT * slot, LANES), BF),
        in_specs=[VMEM],
        out_specs=VMEM,
        scratch_shapes=[pltpu.VMEM((N_CENT * slot, LANES), F32)],
        compiler_params=params(),
        name="final",
    )(got)


def solution(mesh):
    fine = Mesh(mesh.devices.reshape(NX, NZ // 2, 2, NY, NC), ("x", *Z, *CENT))
    pts = ("x", *Z)
    return jax.shard_map(
        body, mesh=fine, in_specs=(P(pts, None), P(CENT, None)), out_specs=P(pts, CENT), check_vma=False
    )
```

```python
import functools

import jax
import jax.numpy as jnp
from jax import lax
from jax.experimental import pallas as pl
from jax.experimental.pallas import tpu as pltpu
from jax.sharding import Mesh, PartitionSpec as P

BF = jnp.bfloat16
F32 = jnp.float32
NX, NZ, NY, NC = 4, 8, 4, 2
Z = ("zq", "zp")
CENT = ("y", "core")
N_CENT = NY * NC
LANES = 128
TAIL = 4
VMEM = pl.BlockSpec(memory_space=pltpu.VMEM)
SMEM = pl.BlockSpec(memory_space=pltpu.SMEM)
ANY = pl.BlockSpec(memory_space=pl.ANY)
WIDE = 58 * 2**20
WIDEST = 125 * 2**19
CHUNKS = 10
CUT = 256


def dot_nt(a, b):
    return lax.dot_general(a, b, (((1,), (1,)), ((), ())), preferred_element_type=F32)


def params(limit=24 * 2**20):
    return pltpu.CompilerParams(vmem_limit_bytes=limit)


def cost(flops, read):
    return pl.CostEstimate(flops=flops, bytes_accessed=read, transcendentals=0)


def cut_kernel(place, points, half_out, eighth_out, sem):
    half, eighth = half_out.shape[0], eighth_out.shape[0]
    a = pltpu.make_async_copy(points.at[pl.ds(pl.multiple_of(place[0] * half, half), half)], half_out, sem.at[0])
    b = pltpu.make_async_copy(
        points.at[pl.ds(pl.multiple_of(place[1] * eighth, eighth), eighth)], eighth_out, sem.at[1]
    )
    a.start()
    b.start()
    a.wait()
    b.wait()


def stats_kernel(points, cents, out, held, sems):
    chunk = held.shape[0] // CHUNKS
    copies = [
        pltpu.make_async_copy(cents.at[pl.ds(i * chunk, chunk)], held.at[pl.ds(i * chunk, chunk)], sems.at[i])
        for i in range(CHUNKS)
    ]
    for copy in copies:
        copy.start()
    pts = points[...]
    tops, totals = [], []
    for i, copy in enumerate(copies):
        copy.wait()
        rows = held[i * chunk : (i + 1) * chunk]
        wide = rows.astype(F32)
        norms = 0.5 * jnp.sum(wide * wide, axis=1, keepdims=True)
        logits = dot_nt(rows, pts) - norms
        top = jnp.max(logits, axis=0, keepdims=True)
        tops.append(top)
        totals.append(jnp.sum(jnp.exp(logits - top), axis=0, keepdims=True))
    top = functools.reduce(jnp.maximum, tops)
    total = sum(s * jnp.exp(t - top) for s, t in zip(totals, tops))
    groups = top.shape[1] // LANES
    tile = jnp.concatenate([r[:, g * LANES : (g + 1) * LANES] for r in (top, total) for g in range(groups)], axis=0)
    out[...] = jnp.broadcast_to(tile[None], out.shape)


def prep_kernel(place, cents, after, rows_out, norms_out, held, sems):
    _, n_rows, _ = rows_out.shape
    n_blocks, window, dim = held.shape
    height = 2 * n_rows // n_blocks
    slot = height - TAIL
    base = place[2] * (n_blocks * slot)
    copies = []
    for b in range(n_blocks):
        at = pl.multiple_of(base + b * slot // 16 * 16, 16)
        copies.append(pltpu.make_async_copy(cents.at[pl.ds(at, window)], held.at[b], sems.at[b]))
    for copy in copies:
        copy.start()
    for q in range(2):
        parts, norms = [], []
        for b in range(q, n_blocks, 2):
            copies[b].wait()
            wide = held[b].astype(F32)[b * slot % 16 :][:slot]
            parts += [wide, jnp.zeros((TAIL, dim), F32)]
            norms += [0.5 * jnp.sum(wide * wide, axis=1, keepdims=True), jnp.full((TAIL, 1), 1e30, F32)]
        rows_out[q] = jnp.concatenate(parts, axis=0).astype(BF)
        norms_out[q] = jnp.concatenate(norms, axis=0)


def lse_of(stats, source):
    groups = stats.shape[1] // 2
    part = stats[pl.ds(source * N_CENT, N_CENT)]
    m, s = part[:, :groups], part[:, groups:]
    high = jnp.max(m, axis=0)
    return high + jnp.log(jnp.sum(s * jnp.exp(m - high[None]), axis=0))


def lse_halves(place, stats, k):
    lse = lse_of(stats, lax.rem(place[2] + NX - k, NX))
    half = lse.shape[0] // 2
    first = place[0] == 0
    return jnp.where(first, lse[:half], lse[half:]), jnp.where(first, lse[half:], lse[:half])


def weighted(pieces, rows, shift, weights):
    counts = jnp.zeros((rows.shape[0], LANES), F32)
    at = 0
    for ref, lse in pieces:
        n = ref.shape[0]
        for c in range(0, n, CUT):
            logits = dot_nt(rows, ref[c : c + CUT])
            for g in range(CUT // LANES):
                row = c // LANES + g
                w = jnp.exp(logits[:, g * LANES : (g + 1) * LANES] - shift - lse[row : row + 1]).astype(BF)
                counts += w.astype(F32)
                weights[:, at + c + g * LANES : at + c + (g + 1) * LANES] = w
        at += n
    numer = None
    at = 0
    for ref, _ in pieces:
        n = ref.shape[0]
        term = jnp.dot(weights[:, at : at + n], ref[...], preferred_element_type=F32)
        numer = term if numer is None else numer + term
        at += n
    return numer, counts


def row_counts(counts, block, height):
    part = counts[block * height : (block + 1) * height]
    part = jnp.concatenate([part, jnp.zeros((LANES - height, LANES), F32)], axis=0)
    return jnp.sum(part.T, axis=0, keepdims=True)


def close(values, first, second):
    height, width = values.shape
    first = jnp.concatenate([first] * (width // LANES), axis=1)
    second = jnp.concatenate([second] * (width // LANES), axis=1)
    last = values[height - 8 :]
    row = lax.broadcasted_iota(jnp.int32, last.shape, 0)
    last = jnp.where(row == 8 - TAIL, first, jnp.where(row == 9 - TAIL, second, jnp.where(row > 9 - TAIL, 0.0, last)))
    return jnp.concatenate([values[: height - 8], last], axis=0)


def split(counts):
    high = counts.astype(BF).astype(F32)
    return high, counts - high


def near_pieces(place, stats, own, a1, a3, b1, b3):
    pieces = [(own, lse_of(stats, place[2]))]
    for k, a, b in ((1, a1, b1), (3, a3, b3)):
        mine, other = lse_halves(place, stats, k)
        pieces += [(a, mine), (b, other)]
    return pieces


def near_kernel(place, stats, rows, norms, own, a1, a3, b1, b3, numer_out, counts_out, weights):
    q = 1 - place[3]
    pieces = near_pieces(place, stats, own, a1, a3, b1, b3)
    numer_out[...], counts_out[...] = weighted(pieces, rows[q], norms[q], weights)


def give_kernel(place, stats, rows, norms, a2, b2, numer, counts, left, right, weights):
    q = 1 - place[3]
    mine, other = lse_halves(place, stats, 2)
    more, more_counts = weighted([(a2, mine), (b2, other)], rows[q], norms[q], weights)
    total, counts = numer[...] + more, counts[...] + more_counts
    blocks, height, width = left.shape
    for b in range(blocks):
        high, low = split(row_counts(counts, b, height))
        values = close(total[b * height : (b + 1) * height], high, low).astype(BF)
        left[b] = values[:, :width]
        right[b] = values[:, width:]


def keep_kernel(place, stats, rows, norms, own, a1, a3, b1, b3, a2, b2, kept, weights):
    q = place[3]
    pieces = near_pieces(place, stats, own, a1, a3, b1, b3)
    mine, other = lse_halves(place, stats, 2)
    numer, counts = weighted(pieces + [(a2, mine), (b2, other)], rows[q], norms[q], weights)
    blocks, height, width = kept.shape
    for b in range(blocks):
        total = row_counts(counts, b, height)
        kept[b] = close(numer[b * height : (b + 1) * height], total, jnp.zeros_like(total))


def merge_kernel(kept, left, right, send):
    blocks, height, width = kept.shape
    at = height - TAIL
    for b in range(blocks):
        for h, got in ((0, left), (1, right)):
            half = width // 2
            mine = kept[b, :, h * half : (h + 1) * half]
            theirs = got[b].astype(F32)
            values = mine + theirs
            tail = values[height - 8 :]
            counts = tail[8 - TAIL : 9 - TAIL, :LANES] + tail[9 - TAIL : 10 - TAIL, :LANES]
            high, low = split(counts)
            values = close(values, high, low).astype(BF)
            for c in range(half // LANES):
                send[b * N_CENT + h * (half // LANES) + c] = values[:, c * LANES : (c + 1) * LANES]


def final_kernel(got, out, scratch):
    n, height, _ = got.shape
    slot = height - TAIL
    for c in range(N_CENT):
        values = got[c].astype(F32)
        for i in range(1, n // N_CENT):
            values += got[i * N_CENT + c].astype(F32)
        tail = values[height - 8 :]
        counts = tail[8 - TAIL : 9 - TAIL] + tail[9 - TAIL : 10 - TAIL] + 1.0
        column = jnp.broadcast_to(counts, (LANES, LANES)).T
        scratch[c * slot : (c + 1) * slot] = (values / column[:height])[:slot]
    out[...] = scratch[...].astype(BF)


def body(points, centroids):
    rows, dim = centroids.shape
    pts = points.shape[0]
    slot = rows // (NX * NZ)
    height = slot + TAIL
    half, eighth = pts // NC, pts // N_CENT
    x, y, parity, core = (lax.axis_index(a) for a in ("x", "y", "zp", "core"))
    place = jnp.stack([core, core * NY + y, x, parity]).astype(jnp.int32)
    shape = jax.ShapeDtypeStruct

    own_half, own_eighth = pl.pallas_call(
        cut_kernel,
        out_shape=(shape((half, dim), BF), shape((eighth, dim), BF)),
        in_specs=[SMEM, ANY],
        out_specs=(VMEM, VMEM),
        scratch_shapes=[pltpu.SemaphoreType.DMA((2,))],
        compiler_params=params(WIDEST),
        cost_estimate=cost(0, 2 * half * dim * 2),
        name="cut",
    )(place, points)

    def ring(a, k):
        return lax.ppermute(a, "x", [(i, (i + k) % NX) for i in range(NX)])

    far = ring(own_eighth, 2)
    near = {1: ring(own_half, 1), 3: ring(own_half, 3)}

    stats_shape = (NX * N_CENT, 2 * pts // LANES, LANES)
    send_stats = pl.pallas_call(
        stats_kernel,
        out_shape=shape(stats_shape, F32),
        in_specs=[VMEM, ANY],
        out_specs=VMEM,
        scratch_shapes=[pltpu.VMEM((rows, dim), BF), pltpu.SemaphoreType.DMA((CHUNKS,))],
        compiler_params=params(WIDE),
        cost_estimate=cost(2 * pts * rows * dim, rows * dim * 2),
        name="stats",
    )(points, centroids)
    stats = lax.all_to_all(send_stats, ("x", *CENT), 0, 0)

    work = NZ // 2 * height
    by_parity, norms = pl.pallas_call(
        prep_kernel,
        out_shape=(shape((2, work, dim), BF), shape((2, work, 1), F32)),
        in_specs=[SMEM, ANY, ANY],
        out_specs=(VMEM, VMEM),
        scratch_shapes=[pltpu.VMEM((NZ, slot + 12, dim), BF), pltpu.SemaphoreType.DMA((NZ,))],
        compiler_params=params(WIDE),
        cost_estimate=cost(0, rows // NX * dim * 2),
        name="prep",
    )(place, centroids, send_stats)

    far, by_parity, norms, stats = lax.optimization_barrier((far, by_parity, norms, stats))
    slices = [far] + [lax.ppermute(far, "y", [(i, i ^ k) for i in range(NY)]) for k in range(1, NY)]
    near, stats = lax.optimization_barrier((near, stats))
    swap = [(0, 1), (1, 0)]
    near_other = {k: lax.ppermute(a, "core", swap) for k, a in near.items()}
    def call(kernel, out_shape, n_points, *args):
        return pl.pallas_call(
            kernel,
            out_shape=out_shape,
            in_specs=[SMEM] + [VMEM] * (3 + len(args)),
            out_specs=jax.tree.map(lambda _: VMEM, out_shape),
            scratch_shapes=[pltpu.VMEM((work, n_points), BF)],
            compiler_params=params(),
            cost_estimate=cost(4 * work * n_points * dim, n_points * dim * 2),
            name=kernel.__name__,
        )(place, stats, by_parity, norms, *args)

    early = (points, near[1], near[3], near_other[1], near_other[3])
    numer = call(near_kernel, (shape((work, dim), F32), shape((work, LANES), F32)), (NX - 1) * pts, *early)
    slices, numer = lax.optimization_barrier((slices, numer))
    slices = jnp.stack(slices)
    a2 = jnp.concatenate([lax.dynamic_index_in_dim(slices, y ^ k, 0, keepdims=False) for k in range(NY)], axis=0)
    b2 = lax.ppermute(a2, "core", swap)
    n_blocks = NZ // 2
    part = shape((n_blocks, height, dim // 2), BF)
    left, right = call(give_kernel, (part, part), pts, a2, b2, *numer)
    got_left = lax.ppermute(left, Z, [(i, i ^ 1) for i in range(NZ)])
    got_right = lax.ppermute(right, Z, [(i, (i + (1 if i % 2 else -1)) % NZ) for i in range(NZ)])
    kept = call(keep_kernel, shape((n_blocks, height, dim), F32), NX * pts, *early, a2, b2)
    send = pl.pallas_call(
        merge_kernel,
        out_shape=shape((n_blocks * N_CENT, height, LANES), BF),
        in_specs=[VMEM] * 3,
        out_specs=VMEM,
        compiler_params=params(),
        name="merge",
    )(kept, got_left, got_right)
    got = lax.all_to_all(send, ("zq", *CENT), 0, 0)
    return pl.pallas_call(
        final_kernel,
        out_shape=shape((N_CENT * slot, LANES), BF),
        in_specs=[VMEM],
        out_specs=VMEM,
        scratch_shapes=[pltpu.VMEM((N_CENT * slot, LANES), F32)],
        compiler_params=params(),
        name="final",
    )(got)


def solution(mesh):
    fine = Mesh(mesh.devices.reshape(NX, NZ // 2, 2, NY, NC), ("x", *Z, *CENT))
    pts = ("x", *Z)
    return jax.shard_map(
        body, mesh=fine, in_specs=(P(pts, None), P(CENT, None)), out_specs=P(pts, CENT), check_vma=False
    )
```

```python
import functools

import jax
import jax.numpy as jnp
from jax import lax
from jax.experimental import pallas as pl
from jax.experimental.pallas import tpu as pltpu
from jax.sharding import Mesh, PartitionSpec as P

BF = jnp.bfloat16
F32 = jnp.float32
NX, NQ, NP, NY, NC = 4, 4, 2, 4, 2
CENT = ("y", "core")
N_CENT = NY * NC
LANES = 128
TAIL = 4
VMEM = pl.BlockSpec(memory_space=pltpu.VMEM)
SMEM = pl.BlockSpec(memory_space=pltpu.SMEM)
ANY = pl.BlockSpec(memory_space=pl.ANY)
MIB = 2**20
CHEAP = pl.CostEstimate(flops=1, bytes_accessed=1, transcendentals=0)
CHUNKS = 5
CUT = 256


def dot_nt(a, b):
    return lax.dot_general(a, b, (((1,), (1,)), ((), ())), preferred_element_type=F32)


def params(mib):
    return pltpu.CompilerParams(vmem_limit_bytes=mib * MIB)


def cut_kernel(place, points, half_out, eighth_out, sem):
    half, eighth = half_out.shape[0], eighth_out.shape[0]
    a = pltpu.make_async_copy(points.at[pl.ds(pl.multiple_of(place[0] * half, half), half)], half_out, sem.at[0])
    b = pltpu.make_async_copy(
        points.at[pl.ds(pl.multiple_of(place[1] * eighth, eighth), eighth)], eighth_out, sem.at[1]
    )
    a.start()
    b.start()
    a.wait()
    b.wait()


def stats_kernel(points, cents, out):
    chunk = cents.shape[0] // CHUNKS
    pts = points[...]
    tops, totals = [], []
    for i in range(CHUNKS):
        rows = cents[i * chunk : (i + 1) * chunk]
        wide = rows.astype(F32)
        norms = 0.5 * jnp.sum(wide * wide, axis=1, keepdims=True)
        logits = dot_nt(rows, pts) - norms
        top = jnp.max(logits, axis=0, keepdims=True)
        tops.append(top)
        totals.append(jnp.sum(jnp.exp(logits - top), axis=0, keepdims=True))
    top = functools.reduce(jnp.maximum, tops)
    total = sum(s * jnp.exp(t - top) for s, t in zip(totals, tops))
    groups = top.shape[1] // LANES
    tile = jnp.concatenate([r[:, g * LANES : (g + 1) * LANES] for r in (top, total) for g in range(groups)], axis=0)
    out[...] = jnp.broadcast_to(tile[None], out.shape)


def prep_kernel(place, cents, after, rows_out, norms_out, held, sems):
    n_blocks, window, dim = held.shape
    slot = rows_out.shape[0] // n_blocks - TAIL
    zq = place[2]
    odd = lax.rem(zq, 2) == 1
    copies = []
    for b in range(n_blocks):
        at = b // NP * (NQ * NP * slot) + (zq * NP + b % NP) * slot
        at = pl.multiple_of(at // 16 * 16, 16)
        copies.append(pltpu.make_async_copy(cents.at[pl.ds(at, window)], held.at[b], sems.at[b]))
    for copy in copies:
        copy.start()
    parts, norms = [], []
    for b in range(n_blocks):
        copies[b].wait()
        wide = held[b].astype(F32)
        even_at, odd_at = b % NP * slot % 16, (NP + b % NP) * slot % 16
        wide = jnp.where(odd, wide[odd_at : odd_at + slot], wide[even_at : even_at + slot])
        parts += [wide, jnp.zeros((TAIL, dim), F32)]
        norms += [0.5 * jnp.sum(wide * wide, axis=1, keepdims=True), jnp.full((TAIL, 1), 1e30, F32)]
    rows_out[...] = jnp.concatenate(parts, axis=0).astype(BF)
    norms_out[...] = jnp.concatenate(norms, axis=0)


def lse_of(stats, source):
    groups = stats.shape[1] // 2
    part = stats[pl.ds(source * N_CENT, N_CENT)]
    m, s = part[:, :groups], part[:, groups:]
    high = jnp.max(m, axis=0)
    return high + jnp.log(jnp.sum(s * jnp.exp(m - high[None]), axis=0))


def lse_halves(place, stats, k):
    lse = lse_of(stats, lax.rem(place[2] + NQ - k, NQ))
    half = lse.shape[0] // 2
    first = place[0] == 0
    return jnp.where(first, lse[:half], lse[half:]), jnp.where(first, lse[half:], lse[:half])


def weighted(pieces, rows, shift, weights):
    counts = jnp.zeros((rows.shape[0], LANES), F32)
    at = 0
    for ref, lse in pieces:
        n = ref.shape[0]
        for c in range(0, n, CUT):
            logits = dot_nt(rows, ref[c : c + CUT])
            for g in range(CUT // LANES):
                row = c // LANES + g
                w = jnp.exp(logits[:, g * LANES : (g + 1) * LANES] - shift - lse[row : row + 1]).astype(BF)
                counts += w.astype(F32)
                weights[:, at + c + g * LANES : at + c + (g + 1) * LANES] = w
        at += n
    numer = None
    at = 0
    for ref, _ in pieces:
        n = ref.shape[0]
        term = jnp.dot(weights[:, at : at + n], ref[...], preferred_element_type=F32)
        numer = term if numer is None else numer + term
        at += n
    return numer, counts


def row_counts(counts, block, height):
    part = counts[block * height : (block + 1) * height]
    part = jnp.concatenate([part, jnp.zeros((LANES - height, LANES), F32)], axis=0)
    return jnp.sum(part.T, axis=0, keepdims=True)


def close(values, first, second):
    height, width = values.shape
    first = jnp.concatenate([first] * (width // LANES), axis=1)
    second = jnp.concatenate([second] * (width // LANES), axis=1)
    last = values[height - 8 :]
    row = lax.broadcasted_iota(jnp.int32, last.shape, 0)
    last = jnp.where(row == 8 - TAIL, first, jnp.where(row == 9 - TAIL, second, jnp.where(row > 9 - TAIL, 0.0, last)))
    return jnp.concatenate([values[: height - 8], last], axis=0)


def split(counts):
    high = counts.astype(BF).astype(F32)
    return high, counts - high


def own_kernel(place, stats, rows, norms, own, numer, counts, weights):
    pieces = [(own, lse_of(stats, place[2]))]
    numer[...], counts[...] = weighted(pieces, rows[...], norms[...], weights)


def far_kernel(place, stats, rows, norms, a, b, numer_in, counts_in, numer, counts, weights):
    mine, other = lse_halves(place, stats, 2)
    more, more_counts = weighted([(a, mine), (b, other)], rows[...], norms[...], weights)
    numer[...], counts[...] = numer_in[...] + more, counts_in[...] + more_counts


def near_pieces(place, stats, up, down, which):
    return [(ref, lse_halves(place, stats, k)[which]) for k, ref in ((1, up), (NQ - 1, down))]


def near_kernel(place, stats, rows, norms, up, down, numer_in, counts_in, numer, counts, weights):
    pieces = near_pieces(place, stats, up, down, 0)
    more, more_counts = weighted(pieces, rows[...], norms[...], weights)
    numer[...], counts[...] = numer_in[...] + more, counts_in[...] + more_counts


def last_kernel(place, stats, rows, norms, up, down, numer_in, counts_in, send, weights):
    pieces = near_pieces(place, stats, up, down, 1)
    more, more_counts = weighted(pieces, rows[...], norms[...], weights)
    numer, counts = numer_in[...] + more, counts_in[...] + more_counts
    n, height, _ = send.shape
    for b in range(n // N_CENT):
        high, low = split(row_counts(counts, b, height))
        values = close(numer[b * height : (b + 1) * height], high, low).astype(BF)
        for c in range(N_CENT):
            send[b * N_CENT + c] = values[:, c * LANES : (c + 1) * LANES]


def final_kernel(got, out, scratch):
    n, height, _ = got.shape
    slot = height - TAIL
    for c in range(N_CENT):
        values = got[c].astype(F32)
        for i in range(1, n // N_CENT):
            values += got[i * N_CENT + c].astype(F32)
        tail = values[height - 8 :]
        counts = tail[8 - TAIL : 9 - TAIL] + tail[9 - TAIL : 10 - TAIL] + 1.0
        column = jnp.broadcast_to(counts, (LANES, LANES)).T
        scratch[c * slot : (c + 1) * slot] = (values / column[:height])[:slot]
    out[...] = scratch[...].astype(BF)


def body(points, centroids):
    rows, dim = centroids.shape
    pts = points.shape[0]
    n_blocks = NX * NP
    slot = rows // (n_blocks * NQ)
    height = slot + TAIL
    half, eighth = pts // NC, pts // N_CENT
    zq, y, core = (lax.axis_index(a) for a in ("zq", "y", "core"))
    place = jnp.stack([core, core * NY + y, zq]).astype(jnp.int32)
    shape = jax.ShapeDtypeStruct

    own_half, own_eighth = pl.pallas_call(
        cut_kernel,
        out_shape=(shape((half, dim), BF), shape((eighth, dim), BF)),
        in_specs=[SMEM, ANY],
        out_specs=(VMEM, VMEM),
        scratch_shapes=[pltpu.SemaphoreType.DMA((2,))],
        compiler_params=params(4),
        cost_estimate=CHEAP,
        name="cut",
    )(place, points)

    def ring(a, k):
        return lax.ppermute(a, "zq", [(i, (i + k) % NQ) for i in range(NQ)])

    far = ring(own_eighth, 2)
    up, down = ring(own_half, 1), ring(own_half, NQ - 1)

    points, own_half, own_eighth = lax.optimization_barrier((points, own_half, own_eighth))
    send_stats = pl.pallas_call(
        stats_kernel,
        out_shape=shape((NQ * N_CENT, 2 * pts // LANES, LANES), F32),
        in_specs=[VMEM, VMEM],
        out_specs=VMEM,
        compiler_params=params(16),
        cost_estimate=CHEAP,
        name="stats",
    )(points, centroids)
    far, _ = lax.optimization_barrier((far, send_stats))
    stats = lax.all_to_all(send_stats, ("zq", *CENT), 0, 0)

    work = n_blocks * height
    mine, norms = pl.pallas_call(
        prep_kernel,
        out_shape=(shape((work, dim), BF), shape((work, 1), F32)),
        in_specs=[SMEM, ANY, ANY],
        out_specs=(VMEM, VMEM),
        scratch_shapes=[pltpu.VMEM((n_blocks, slot + 12, dim), BF), pltpu.SemaphoreType.DMA((n_blocks,))],
        compiler_params=params(16),
        cost_estimate=CHEAP,
        name="prep",
    )(place, centroids, send_stats)

    def call(kernel, out_shape, *args):
        return pl.pallas_call(
            kernel,
            out_shape=out_shape,
            in_specs=[SMEM] + [VMEM] * (3 + len(args)),
            out_specs=jax.tree.map(lambda _: VMEM, out_shape),
            scratch_shapes=[pltpu.VMEM((work, pts), BF)],
            compiler_params=params(24),
            cost_estimate=CHEAP,
            name=kernel.__name__,
        )(place, stats, mine, norms, *args)

    sums = (shape((work, dim), F32), shape((work, LANES), F32))
    swap = [(0, 1), (1, 0)]

    slices = [far] + [lax.ppermute(far, "y", [(i, i ^ k) for i in range(NY)]) for k in range(1, NY)]
    up, down, stats = lax.optimization_barrier((up, down, stats))
    other_up, other_down = (lax.ppermute(a, "core", swap) for a in (up, down))
    numer = call(own_kernel, sums, points)
    slices, numer = lax.optimization_barrier((slices, numer))
    slices = jnp.stack(slices)
    far = jnp.concatenate([lax.dynamic_index_in_dim(slices, y ^ k, 0, keepdims=False) for k in range(NY)], axis=0)
    other_far = lax.ppermute(far, "core", swap)
    numer = call(near_kernel, sums, up, down, *numer)
    numer = call(far_kernel, sums, far, other_far, *numer)
    send = call(last_kernel, shape((n_blocks * N_CENT, height, LANES), BF), other_up, other_down, *numer)
    got = lax.all_to_all(send, ("x", "zp", *CENT), 0, 0)
    return pl.pallas_call(
        final_kernel,
        out_shape=shape((N_CENT * slot, LANES), BF),
        in_specs=[VMEM],
        out_specs=VMEM,
        scratch_shapes=[pltpu.VMEM((N_CENT * slot, LANES), F32)],
        compiler_params=params(16),
        name="final",
    )(got)


def solution(mesh):
    fine = Mesh(mesh.devices.reshape(NX, NQ, NP, NY, NC), ("x", "zq", "zp", *CENT))
    pts = ("x", "zq", "zp")
    return jax.shard_map(
        body, mesh=fine, in_specs=(P(pts, None), P(CENT, None)), out_specs=P(pts, CENT), check_vma=False
    )
```

```python
import functools

import jax
import jax.numpy as jnp
from jax import lax
from jax.experimental import pallas as pl
from jax.experimental.pallas import tpu as pltpu
from jax.sharding import Mesh, PartitionSpec as P

BF = jnp.bfloat16
F32 = jnp.float32
NX, NQ, NP, NY, NC = 4, 4, 2, 4, 2
CENT = ("y", "core")
N_CENT = NY * NC
LANES = 128
TAIL = 4
VMEM = pl.BlockSpec(memory_space=pltpu.VMEM)
SMEM = pl.BlockSpec(memory_space=pltpu.SMEM)
ANY = pl.BlockSpec(memory_space=pl.ANY)
MIB = 2**20
CHEAP = pl.CostEstimate(flops=1, bytes_accessed=1, transcendentals=0)
TILE = 640
CUT = 256


def dot_nt(a, b):
    return lax.dot_general(a, b, (((1,), (1,)), ((), ())), preferred_element_type=F32)


def params(mib):
    return pltpu.CompilerParams(vmem_limit_bytes=mib * MIB)


def cut_kernel(place, points, half_out, eighth_out, sem):
    half, eighth = half_out.shape[0], eighth_out.shape[0]
    a = pltpu.make_async_copy(points.at[pl.ds(pl.multiple_of(place[0] * half, half), half)], half_out, sem.at[0])
    b = pltpu.make_async_copy(
        points.at[pl.ds(pl.multiple_of(place[1] * eighth, eighth), eighth)], eighth_out, sem.at[1]
    )
    a.start()
    b.start()
    a.wait()
    b.wait()


def stats_kernel(place, points, cents, table, out, mine, top, total, sems):
    step = pl.program_id(0)
    count = NX
    window = mine.shape[0] // count
    stride = table.shape[0] // count
    start = pl.multiple_of(place[2] * (stride // NQ) // 16 * 16, 16)
    copies = [
        pltpu.make_async_copy(table.at[pl.ds(i * stride + start, window)], mine.at[pl.ds(i * window, window)], sems.at[i])
        for i in range(count)
    ]

    @pl.when(step == 0)
    def _():
        for copy in copies:
            copy.start()
        top[...] = jnp.full_like(top, -jnp.inf)
        total[...] = jnp.zeros_like(total)

    rows = cents[...]
    chunk = rows.shape[0] // 2
    pts = points[...]
    tops, totals = [top[...]], [total[...]]
    for i in range(2):
        part = rows[i * chunk : (i + 1) * chunk]
        wide = part.astype(F32)
        logits = dot_nt(part, pts) - 0.5 * jnp.sum(wide * wide, axis=1, keepdims=True)
        high = jnp.max(logits, axis=0, keepdims=True)
        tops.append(high)
        totals.append(jnp.sum(jnp.exp(logits - high), axis=0, keepdims=True))
    new = functools.reduce(jnp.maximum, tops)
    top[...] = new
    total[...] = sum(s * jnp.exp(t - new) for s, t in zip(totals, tops))

    @pl.when(step == pl.num_programs(0) - 1)
    def _():
        groups = top.shape[1] // LANES
        both = [r[:, g * LANES : (g + 1) * LANES] for r in (top[...], total[...]) for g in range(groups)]
        out[...] = jnp.broadcast_to(jnp.concatenate(both, axis=0)[None], out.shape)
        for copy in copies:
            copy.wait()


def lse_of(stats, source):
    groups = stats.shape[1] // 2
    part = stats[pl.ds(source * N_CENT, N_CENT)]
    m, s = part[:, :groups], part[:, groups:]
    high = jnp.max(m, axis=0)
    return high + jnp.log(jnp.sum(s * jnp.exp(m - high[None]), axis=0))


def lse_halves(place, stats, k):
    lse = lse_of(stats, lax.rem(place[2] + NQ - k, NQ))
    half = lse.shape[0] // 2
    first = place[0] == 0
    return jnp.where(first, lse[:half], lse[half:]), jnp.where(first, lse[half:], lse[:half])


def weighted(pieces, rows, shift, weights):
    counts = jnp.zeros((rows.shape[0], LANES), F32)
    at = 0
    for ref, lse in pieces:
        n = ref.shape[0]
        for c in range(0, n, CUT):
            logits = dot_nt(rows, ref[c : c + CUT])
            for g in range(CUT // LANES):
                row = c // LANES + g
                w = jnp.exp(logits[:, g * LANES : (g + 1) * LANES] - shift - lse[row : row + 1]).astype(BF)
                counts += w.astype(F32)
                weights[:, at + c + g * LANES : at + c + (g + 1) * LANES] = w
        at += n
    numer = None
    at = 0
    for ref, _ in pieces:
        n = ref.shape[0]
        term = jnp.dot(weights[:, at : at + n], ref[...], preferred_element_type=F32)
        numer = term if numer is None else numer + term
        at += n
    return numer, counts


def row_counts(part):
    part = jnp.concatenate([part, jnp.zeros((LANES - part.shape[0], LANES), F32)], axis=0)
    return jnp.sum(part.T, axis=0, keepdims=True)


def close(values, first, second):
    height, width = values.shape
    first = jnp.concatenate([first] * (width // LANES), axis=1)
    second = jnp.concatenate([second] * (width // LANES), axis=1)
    last = values[height - 8 :]
    row = lax.broadcasted_iota(jnp.int32, last.shape, 0)
    last = jnp.where(row == 8 - TAIL, first, jnp.where(row == 9 - TAIL, second, jnp.where(row > 9 - TAIL, 0.0, last)))
    return jnp.concatenate([values[: height - 8], last], axis=0)


def split(counts):
    high = counts.astype(BF).astype(F32)
    return high, counts - high


def own_kernel(place, stats, rows, own, numer, counts, norms, weights):
    values = rows[...]
    wide = values.astype(F32)
    shift = 0.5 * jnp.sum(wide * wide, axis=1, keepdims=True)
    norms[...] = shift
    numer[...], counts[...] = weighted([(own, lse_of(stats, place[2]))], values, shift, weights)


def half_pieces(place, stats, up, down, far, which):
    lse = lse_halves(place, stats, 2)[which]
    y = place[3]
    lse = jnp.where(lax.rem(y, 2) == 1, jnp.concatenate([lse[:, LANES // 2 :], lse[:, : LANES // 2]], axis=1), lse)
    lse = jnp.where(y >= 2, jnp.concatenate([lse[1:], lse[:1]], axis=0), lse)
    pieces = [(ref, lse_halves(place, stats, k)[which]) for k, ref in ((1, up), (NQ - 1, down))]
    return [(far, lse)] + pieces


def first_kernel(place, stats, rows, norms, up, down, far, numer_in, counts_in, numer, counts, weights):
    pieces = half_pieces(place, stats, up, down, far, 0)
    more, more_counts = weighted(pieces, rows[...], norms[...], weights)
    numer[...], counts[...] = numer_in[...] + more, counts_in[...] + more_counts


def second_kernel(place, stats, rows, norms, up, down, far, numer_in, counts_in, send, weights, numer, counts):
    pieces = half_pieces(place, stats, up, down, far, 1)
    more, more_counts = weighted(pieces, rows[...], norms[...], weights)
    numer[...], counts[...] = numer_in[...] + more, counts_in[...] + more_counts
    n, height, _ = send.shape
    slot = height - TAIL
    window = rows.shape[0] // NX
    skip = lax.rem(place[2], 2) * 8
    for b in range(n // N_CENT):
        at = b % NP * slot
        start = pl.multiple_of(b // NP * window + skip + at // 8 * 8, 8)
        off = at % 8
        values = numer[pl.ds(start, height)]
        some = counts[pl.ds(start, height)]
        if off:
            values = jnp.concatenate([values[off:], values[:off]], axis=0)
            some = jnp.concatenate([some[off:], some[:off]], axis=0)
        high, low = split(row_counts(some))
        values = close(values, high, low).astype(BF)
        for c in range(N_CENT):
            send[b * N_CENT + c] = values[:, c * LANES : (c + 1) * LANES]


def final_kernel(got, out, scratch):
    n, height, _ = got.shape
    slot = height - TAIL
    for c in range(N_CENT):
        values = got[c].astype(F32)
        for i in range(1, n // N_CENT):
            values += got[i * N_CENT + c].astype(F32)
        tail = values[height - 8 :]
        counts = tail[8 - TAIL : 9 - TAIL] + tail[9 - TAIL : 10 - TAIL] + 1.0
        column = jnp.broadcast_to(counts, (LANES, LANES)).T
        scratch[c * slot : (c + 1) * slot] = (values / column[:height])[:slot]
    out[...] = scratch[...].astype(BF)


def body(points, centroids):
    rows, dim = centroids.shape
    pts = points.shape[0]
    n_blocks = NX * NP
    slot = rows // (n_blocks * NQ)
    height = slot + TAIL
    half, eighth = pts // NC, pts // N_CENT
    zq, y, core = (lax.axis_index(a) for a in ("zq", "y", "core"))
    place = jnp.stack([core, core * NY + y, zq, y]).astype(jnp.int32)
    shape = jax.ShapeDtypeStruct

    own_half, own_eighth = pl.pallas_call(
        cut_kernel,
        out_shape=(shape((half, dim), BF), shape((eighth, dim), BF)),
        in_specs=[SMEM, ANY],
        out_specs=(ANY, ANY),
        scratch_shapes=[pltpu.SemaphoreType.DMA((2,))],
        compiler_params=params(62),
        cost_estimate=CHEAP,
        name="cut",
    )(place, points)

    def ring(a, k):
        return lax.ppermute(a, "zq", [(i, (i + k) % NQ) for i in range(NQ)])

    far = ring(own_eighth, 2)
    up, down = ring(own_half, 1), ring(own_half, NQ - 1)

    points, own_half, own_eighth = lax.optimization_barrier((points, own_half, own_eighth))
    window = -(-(rows // (NX * NQ)) // 16) * 16
    work = NX * window
    stats_shape = (NQ * N_CENT, 2 * pts // LANES, LANES)
    send_stats, mine = pl.pallas_call(
        stats_kernel,
        grid=(rows // TILE,),
        out_shape=(shape(stats_shape, F32), shape((work, dim), BF)),
        in_specs=[
            SMEM,
            pl.BlockSpec((pts, dim), lambda i: (0, 0)),
            pl.BlockSpec((TILE, dim), lambda i: (i, 0)),
            ANY,
        ],
        out_specs=(pl.BlockSpec(stats_shape, lambda i: (0, 0, 0)), ANY),
        scratch_shapes=[pltpu.VMEM((1, pts), F32), pltpu.VMEM((1, pts), F32), pltpu.SemaphoreType.DMA((NX,))],
        compiler_params=params(57),
        cost_estimate=CHEAP,
        name="stats",
    )(place, points, centroids, centroids)
    far, _ = lax.optimization_barrier((far, send_stats))
    stats = lax.all_to_all(send_stats, ("zq", *CENT), 0, 0)

    def call(kernel, out_shape, n_points, *args, scratch=()):
        return pl.pallas_call(
            kernel,
            out_shape=out_shape,
            in_specs=[SMEM] + [VMEM] * (2 + len(args)),
            out_specs=jax.tree.map(lambda _: VMEM, out_shape),
            scratch_shapes=[pltpu.VMEM((work, n_points), BF), *scratch],
            compiler_params=params(28),
            cost_estimate=CHEAP,
            name=kernel.__name__,
        )(place, stats, mine, *args)

    swap = [(0, 1), (1, 0)]
    slices = [far] + [lax.ppermute(far, "y", [(i, i ^ k) for i in range(NY)]) for k in range(1, NY)]
    up, down, stats = lax.optimization_barrier((up, down, stats))
    others = [lax.ppermute(a, "core", swap) for a in (up, down)]
    sums = (shape((work, dim), F32), shape((work, LANES), F32))
    *numer, norms = call(own_kernel, (*sums, shape((work, 1), F32)), pts, points)
    slices, numer = lax.optimization_barrier((slices, numer))
    far = jnp.concatenate(slices, axis=0)
    others.append(lax.ppermute(far, "core", swap))
    more = (NQ - 1) * half
    numer = call(first_kernel, sums, more, norms, up, down, far, *numer)
    send = call(
        second_kernel,
        shape((n_blocks * N_CENT, height, LANES), BF),
        more,
        norms,
        *others,
        *numer,
        scratch=[pltpu.VMEM(s.shape, F32) for s in sums],
    )
    got = lax.all_to_all(send, ("x", "zp", *CENT), 0, 0)
    return pl.pallas_call(
        final_kernel,
        out_shape=shape((N_CENT * slot, LANES), BF),
        in_specs=[VMEM],
        out_specs=VMEM,
        scratch_shapes=[pltpu.VMEM((N_CENT * slot, LANES), F32)],
        compiler_params=params(16),
        name="final",
    )(got)


def solution(mesh):
    fine = Mesh(mesh.devices.reshape(NX, NQ, NP, NY, NC), ("x", "zq", "zp", *CENT))
    pts = ("x", "zq", "zp")
    return jax.shard_map(
        body, mesh=fine, in_specs=(P(pts, None), P(CENT, None)), out_specs=P(pts, CENT), check_vma=False
    )
```

```python
import functools

import jax
import jax.numpy as jnp
from jax import lax
from jax.experimental import pallas as pl
from jax.experimental.pallas import tpu as pltpu
from jax.sharding import Mesh, PartitionSpec as P

BF = jnp.bfloat16
F32 = jnp.float32
NX, NQ, NP, NY, NC = 4, 4, 2, 4, 2
CENT = ("y", "core")
N_CENT = NY * NC
LANES = 128
TAIL = 4
VMEM = pl.BlockSpec(memory_space=pltpu.VMEM)
SMEM = pl.BlockSpec(memory_space=pltpu.SMEM)
ANY = pl.BlockSpec(memory_space=pl.ANY)
MIB = 2**20
CHEAP = pl.CostEstimate(flops=1, bytes_accessed=1, transcendentals=0)
TILE = 640
CUT = 256


def dot_nt(a, b):
    return lax.dot_general(a, b, (((1,), (1,)), ((), ())), preferred_element_type=F32)


def params(mib):
    return pltpu.CompilerParams(vmem_limit_bytes=mib * MIB)


def cut_kernel(place, points, half_out, eighth_out):
    half, eighth = half_out.shape[0], eighth_out.shape[0]
    half_out[...] = points[pl.ds(pl.multiple_of(place[0] * half, half), half)]
    eighth_out[...] = points[pl.ds(pl.multiple_of(place[1] * eighth, eighth), eighth)]


def stats_kernel(points, cents, out, top, total):
    step = pl.program_id(0)

    @pl.when(step == 0)
    def _():
        top[...] = jnp.full_like(top, -jnp.inf)
        total[...] = jnp.zeros_like(total)

    rows = cents[...]
    chunk = rows.shape[0] // 2
    pts = points[...]
    tops, totals = [top[...]], [total[...]]
    for i in range(2):
        part = rows[i * chunk : (i + 1) * chunk]
        wide = part.astype(F32)
        logits = dot_nt(part, pts) - 0.5 * jnp.sum(wide * wide, axis=1, keepdims=True)
        high = jnp.max(logits, axis=0, keepdims=True)
        tops.append(high)
        totals.append(jnp.sum(jnp.exp(logits - high), axis=0, keepdims=True))
    new = functools.reduce(jnp.maximum, tops)
    top[...] = new
    total[...] = sum(s * jnp.exp(t - new) for s, t in zip(totals, tops))

    @pl.when(step == pl.num_programs(0) - 1)
    def _():
        groups = top.shape[1] // LANES
        both = [r[:, g * LANES : (g + 1) * LANES] for r in (top[...], total[...]) for g in range(groups)]
        out[...] = jnp.broadcast_to(jnp.concatenate(both, axis=0)[None], out.shape)


def window_kernel(place, table, after, mine, norms, sems):
    window = mine.shape[0] // NX
    stride = table.shape[0] // NX
    start = pl.multiple_of(place[2] * (stride // NQ) // 16 * 16, 16)
    copies = [
        pltpu.make_async_copy(table.at[pl.ds(i * stride + start, window)], mine.at[pl.ds(i * window, window)], sems.at[i])
        for i in range(NX)
    ]
    for copy in copies:
        copy.start()
    for i, copy in enumerate(copies):
        copy.wait()
        wide = mine[i * window : (i + 1) * window].astype(F32)
        norms[i * window : (i + 1) * window] = 0.5 * jnp.sum(wide * wide, axis=1, keepdims=True)


def lse_of(stats, source):
    groups = stats.shape[1] // 2
    part = stats[pl.ds(source * N_CENT, N_CENT)]
    m, s = part[:, :groups], part[:, groups:]
    high = jnp.max(m, axis=0)
    return high + jnp.log(jnp.sum(s * jnp.exp(m - high[None]), axis=0))


def lse_halves(place, stats, k):
    lse = lse_of(stats, lax.rem(place[2] + NQ - k, NQ))
    half = lse.shape[0] // 2
    first = place[0] == 0
    return jnp.where(first, lse[:half], lse[half:]), jnp.where(first, lse[half:], lse[:half])


def weighted(pieces, rows, shift, weights, held):
    counts = jnp.zeros((rows.shape[0], LANES), F32)
    at = 0
    for ref, lse in pieces:
        n = ref.shape[0]
        for c in range(0, n, CUT):
            block = ref[c : c + CUT]
            if held is not None:
                held[at + c : at + c + CUT] = block
            logits = dot_nt(rows, block)
            for g in range(CUT // LANES):
                row = c // LANES + g
                w = jnp.exp(logits[:, g * LANES : (g + 1) * LANES] - shift - lse[row : row + 1]).astype(BF)
                counts += w.astype(F32)
                weights[:, at + c + g * LANES : at + c + (g + 1) * LANES] = w
        at += n
    source = pieces[0][0] if held is None else held
    return jnp.dot(weights[...], source[...], preferred_element_type=F32), counts


def row_counts(part):
    part = jnp.concatenate([part, jnp.zeros((LANES - part.shape[0], LANES), F32)], axis=0)
    return jnp.sum(part.T, axis=0, keepdims=True)


def close(values, first, second):
    height, width = values.shape
    first = jnp.concatenate([first] * (width // LANES), axis=1)
    second = jnp.concatenate([second] * (width // LANES), axis=1)
    last = values[height - 8 :]
    row = lax.broadcasted_iota(jnp.int32, last.shape, 0)
    last = jnp.where(row == 8 - TAIL, first, jnp.where(row == 9 - TAIL, second, jnp.where(row > 9 - TAIL, 0.0, last)))
    return jnp.concatenate([values[: height - 8], last], axis=0)


def split(counts):
    high = counts.astype(BF).astype(F32)
    return high, counts - high


def own_kernel(place, stats, rows, norms, own, numer, counts, weights):
    pieces = [(own, lse_of(stats, place[2]))]
    numer[...], counts[...] = weighted(pieces, rows[...], norms[...], weights, None)


def half_pieces(place, stats, up, down, far, which):
    lse = lse_halves(place, stats, 2)[which]
    y = place[3]
    lse = jnp.where(lax.rem(y, 2) == 1, jnp.concatenate([lse[:, LANES // 2 :], lse[:, : LANES // 2]], axis=1), lse)
    lse = jnp.where(y >= 2, jnp.concatenate([lse[1:], lse[:1]], axis=0), lse)
    pieces = [(ref, lse_halves(place, stats, k)[which]) for k, ref in ((1, up), (NQ - 1, down))]
    return [(far, lse)] + pieces


def first_kernel(place, stats, rows, norms, up, down, far, numer_in, counts_in, numer, counts, weights, held):
    pieces = half_pieces(place, stats, up, down, far, 0)
    more, more_counts = weighted(pieces, rows[...], norms[...], weights, held)
    numer[...], counts[...] = numer_in[...] + more, counts_in[...] + more_counts


def second_kernel(place, stats, rows, norms, up, down, far, numer_in, counts_in, send, weights, held, numer, counts):
    pieces = half_pieces(place, stats, up, down, far, 1)
    more, more_counts = weighted(pieces, rows[...], norms[...], weights, held)
    numer[...], counts[...] = numer_in[...] + more, counts_in[...] + more_counts
    n, height, _ = send.shape
    slot = height - TAIL
    window = rows.shape[0] // NX
    skip = lax.rem(place[2], 2) * 8
    for b in range(n // N_CENT):
        at = b % NP * slot
        start = pl.multiple_of(b // NP * window + skip + at // 8 * 8, 8)
        off = at % 8
        values = numer[pl.ds(start, height)]
        some = counts[pl.ds(start, height)]
        if off:
            values = jnp.concatenate([values[off:], values[:off]], axis=0)
            some = jnp.concatenate([some[off:], some[:off]], axis=0)
        high, low = split(row_counts(some))
        values = close(values, high, low).astype(BF)
        for c in range(N_CENT):
            send[b * N_CENT + c] = values[:, c * LANES : (c + 1) * LANES]


def final_kernel(got, out, scratch):
    n, height, _ = got.shape
    slot = height - TAIL
    for c in range(N_CENT):
        values = got[c].astype(F32)
        for i in range(1, n // N_CENT):
            values += got[i * N_CENT + c].astype(F32)
        tail = values[height - 8 :]
        counts = tail[8 - TAIL : 9 - TAIL] + tail[9 - TAIL : 10 - TAIL] + 1.0
        column = jnp.broadcast_to(counts, (LANES, LANES)).T
        scratch[c * slot : (c + 1) * slot] = (values / column[:height])[:slot]
    out[...] = scratch[...].astype(BF)


def body(points, centroids):
    rows, dim = centroids.shape
    pts = points.shape[0]
    n_blocks = NX * NP
    slot = rows // (n_blocks * NQ)
    height = slot + TAIL
    half, eighth = pts // NC, pts // N_CENT
    zq, y, core = (lax.axis_index(a) for a in ("zq", "y", "core"))
    place = jnp.stack([core, core * NY + y, zq, y]).astype(jnp.int32)
    shape = jax.ShapeDtypeStruct

    own_half, own_eighth = pl.pallas_call(
        cut_kernel,
        out_shape=(shape((half, dim), BF), shape((eighth, dim), BF)),
        in_specs=[SMEM, VMEM],
        out_specs=(VMEM, VMEM),
        compiler_params=params(4),
        cost_estimate=CHEAP,
        name="cut",
    )(place, points)

    def ring(a, k):
        return lax.ppermute(a, "zq", [(i, (i + k) % NQ) for i in range(NQ)])

    far = ring(own_eighth, 2)
    up, down = ring(own_half, 1), ring(own_half, NQ - 1)

    points, own_half, own_eighth = lax.optimization_barrier((points, own_half, own_eighth))
    window = -(-(rows // (NX * NQ)) // 16) * 16
    work = NX * window
    stats_shape = (NQ * N_CENT, 2 * pts // LANES, LANES)
    send_stats = pl.pallas_call(
        stats_kernel,
        grid=(rows // TILE,),
        out_shape=shape(stats_shape, F32),
        in_specs=[pl.BlockSpec((pts, dim), lambda i: (0, 0)), pl.BlockSpec((TILE, dim), lambda i: (i, 0))],
        out_specs=pl.BlockSpec(stats_shape, lambda i: (0, 0, 0)),
        scratch_shapes=[pltpu.VMEM((1, pts), F32), pltpu.VMEM((1, pts), F32)],
        compiler_params=params(54),
        cost_estimate=CHEAP,
        name="stats",
    )(points, centroids)
    far, _ = lax.optimization_barrier((far, send_stats))
    stats = lax.all_to_all(send_stats, ("zq", *CENT), 0, 0)
    mine, norms = pl.pallas_call(
        window_kernel,
        out_shape=(shape((work, dim), BF), shape((work, 1), F32)),
        in_specs=[SMEM, ANY, ANY],
        out_specs=(VMEM, VMEM),
        scratch_shapes=[pltpu.SemaphoreType.DMA((NX,))],
        compiler_params=params(50),
        cost_estimate=CHEAP,
        name="window",
    )(place, centroids, send_stats)

    def call(kernel, out_shape, n_points, *args, scratch=()):
        return pl.pallas_call(
            kernel,
            out_shape=out_shape,
            in_specs=[SMEM] + [VMEM] * (3 + len(args)),
            out_specs=jax.tree.map(lambda _: VMEM, out_shape),
            scratch_shapes=[pltpu.VMEM((work, n_points), BF), *scratch],
            compiler_params=params(28),
            cost_estimate=CHEAP,
            name=kernel.__name__,
        )(place, stats, mine, norms, *args)

    swap = [(0, 1), (1, 0)]
    slices = [far] + [lax.ppermute(far, "y", [(i, i ^ k) for i in range(NY)]) for k in range(1, NY)]
    up, down, stats = lax.optimization_barrier((up, down, stats))
    others = [lax.ppermute(a, "core", swap) for a in (up, down)]
    sums = (shape((work, dim), F32), shape((work, LANES), F32))
    numer = call(own_kernel, sums, pts, points)
    slices, numer = lax.optimization_barrier((slices, numer))
    far = jnp.concatenate(slices, axis=0)
    others.append(lax.ppermute(far, "core", swap))
    more = (NQ - 1) * half
    held = pltpu.VMEM((more, dim), BF)
    numer = call(first_kernel, sums, more, up, down, far, *numer, scratch=[held])
    send = call(
        second_kernel,
        shape((n_blocks * N_CENT, height, LANES), BF),
        more,
        *others,
        *numer,
        scratch=[held, *(pltpu.VMEM(s.shape, F32) for s in sums)],
    )
    got = lax.all_to_all(send, ("x", "zp", *CENT), 0, 0)
    return pl.pallas_call(
        final_kernel,
        out_shape=shape((N_CENT * slot, LANES), BF),
        in_specs=[VMEM],
        out_specs=VMEM,
        scratch_shapes=[pltpu.VMEM((N_CENT * slot, LANES), F32)],
        compiler_params=params(16),
        name="final",
    )(got)


def solution(mesh):
    fine = Mesh(mesh.devices.reshape(NX, NQ, NP, NY, NC), ("x", "zq", "zp", *CENT))
    pts = ("x", "zq", "zp")
    return jax.shard_map(
        body, mesh=fine, in_specs=(P(pts, None), P(CENT, None)), out_specs=P(pts, CENT), check_vma=False
    )
```

```python
import functools

import jax
import jax.numpy as jnp
from jax import lax
from jax.experimental import pallas as pl
from jax.experimental.pallas import tpu as pltpu
from jax.sharding import Mesh, PartitionSpec as P

BF = jnp.bfloat16
F32 = jnp.float32
NX, NZ, NY, NC = 4, 8, 4, 2
Z = ("zq", "zp")
CENT = ("y", "core")
N_CENT = NY * NC
LANES = 128
TAIL = 4
VMEM = pl.BlockSpec(memory_space=pltpu.VMEM)
SMEM = pl.BlockSpec(memory_space=pltpu.SMEM)
ANY = pl.BlockSpec(memory_space=pl.ANY)
MIB = 2**20
CHEAP = pl.CostEstimate(flops=1, bytes_accessed=1, transcendentals=0)
TILE = 640


def dot_nt(a, b):
    return lax.dot_general(a, b, (((1,), (1,)), ((), ())), preferred_element_type=F32)


def params(mib):
    return pltpu.CompilerParams(vmem_limit_bytes=mib * MIB)


def cut_kernel(place, points, half_out, part_out):
    half, part = half_out.shape[0], part_out.shape[0]
    half_out[...] = points[pl.ds(pl.multiple_of(place[0] * half, half), half)]
    part_out[...] = points[pl.ds(pl.multiple_of(place[1] * part, part), part)]


def stats_kernel(points, cents, out, top, total):
    step = pl.program_id(0)

    @pl.when(step == 0)
    def _():
        top[...] = jnp.full_like(top, -jnp.inf)
        total[...] = jnp.zeros_like(total)

    rows = cents[...]
    chunk = rows.shape[0] // 2
    pts = points[...]
    tops, totals = [top[...]], [total[...]]
    for i in range(2):
        part = rows[i * chunk : (i + 1) * chunk]
        wide = part.astype(F32)
        logits = dot_nt(part, pts) - 0.5 * jnp.sum(wide * wide, axis=1, keepdims=True)
        high = jnp.max(logits, axis=0, keepdims=True)
        tops.append(high)
        totals.append(jnp.sum(jnp.exp(logits - high), axis=0, keepdims=True))
    new = functools.reduce(jnp.maximum, tops)
    top[...] = new
    total[...] = sum(s * jnp.exp(t - new) for s, t in zip(totals, tops))

    @pl.when(step == pl.num_programs(0) - 1)
    def _():
        groups = top.shape[1] // LANES
        both = [r[:, g * LANES : (g + 1) * LANES] for r in (top[...], total[...]) for g in range(groups)]
        out[...] = jnp.broadcast_to(jnp.concatenate(both, axis=0)[None], out.shape)


def window_kernel(place, table, after, mine, norms, sems):
    _, work, _ = mine.shape
    count = NZ // 2
    window = work // count
    stride = table.shape[0] // NX
    slot = stride // NZ
    copies = {}
    for q in range(2):
        for i in range(count):
            at = pl.multiple_of(place[2] * stride + (2 * i + q) * slot // 16 * 16, 16)
            to = mine.at[q, pl.ds(i * window, window)]
            copies[q, i] = pltpu.make_async_copy(table.at[pl.ds(at, window)], to, sems.at[q * count + i])
    for copy in copies.values():
        copy.start()
    for (q, i), copy in copies.items():
        copy.wait()
        here = slice(i * window, (i + 1) * window)
        wide = mine[q, here].astype(F32)
        norms[q, here] = 0.5 * jnp.sum(wide * wide, axis=1, keepdims=True)


def lse_of(stats, source):
    groups = stats.shape[1] // 2
    part = stats[pl.ds(source * N_CENT, N_CENT)]
    m, s = part[:, :groups], part[:, groups:]
    high = jnp.max(m, axis=0)
    return high + jnp.log(jnp.sum(s * jnp.exp(m - high[None]), axis=0))


def lse_halves(place, stats, k):
    lse = lse_of(stats, lax.rem(place[2] + NX - k, NX))
    half = lse.shape[0] // 2
    first = place[0] == 0
    return jnp.where(first, lse[:half], lse[half:]), jnp.where(first, lse[half:], lse[:half])


def weighted(pieces, rows, norms, q, held, numer, counts, before=None):
    at = 0
    lse = []
    for ref, part in pieces:
        held[at : at + ref.shape[0]] = ref[...]
        lse += [part[g : g + 1] for g in range(part.shape[0])]
        at += ref.shape[0]
    logits = dot_nt(rows[q], held[...])
    shift = norms[q]
    some = jnp.zeros(counts.shape, F32)
    weights = []
    for g, part in enumerate(lse):
        w = jnp.exp(logits[:, g * LANES : (g + 1) * LANES] - shift - part).astype(BF)
        some += w.astype(F32)
        weights.append(w)
    more = jnp.dot(jnp.concatenate(weights, axis=1), held[...], preferred_element_type=F32)
    if before is not None:
        more, some = before[0][...] + more, before[1][...] + some
    numer[...] = more
    counts[...] = some


def block_of(numer, counts, i, q, height):
    start = i * (numer.shape[0] * 2 // NZ) + 8 * (i % 2)
    found = []
    for ref in (numer, counts):
        v = ref[start : start + height]
        found.append(jnp.where(q == 1, jnp.concatenate([v[4:], v[:4]], axis=0), v))
    return found[0], row_counts(found[1])


def row_counts(part):
    part = jnp.concatenate([part, jnp.zeros((LANES - part.shape[0], LANES), F32)], axis=0)
    return jnp.sum(part.T, axis=0, keepdims=True)


def close(values, first, second):
    height, width = values.shape
    first = jnp.concatenate([first] * (width // LANES), axis=1)
    second = jnp.concatenate([second] * (width // LANES), axis=1)
    last = values[height - 8 :]
    row = lax.broadcasted_iota(jnp.int32, last.shape, 0)
    last = jnp.where(row == 8 - TAIL, first, jnp.where(row == 9 - TAIL, second, jnp.where(row > 9 - TAIL, 0.0, last)))
    return jnp.concatenate([values[: height - 8], last], axis=0)


def split(counts):
    high = counts.astype(BF).astype(F32)
    return high, counts - high


def own_kernel(place, stats, rows, norms, own, numer, counts, held):
    weighted([(own, lse_of(stats, place[2]))], rows, norms, 1 - place[3], held, numer, counts)


def near_pieces(place, stats, up, down, other_up, other_down):
    pieces = []
    for k, a, b in ((1, up, other_up), (NX - 1, down, other_down)):
        mine, other = lse_halves(place, stats, k)
        pieces += [(a, mine), (b, other)]
    return pieces


def far_pieces(place, stats, slices):
    lse = lse_of(stats, lax.rem(place[2] + 2, NX))
    y = place[1]
    pieces = []
    for k, ref in enumerate(slices):
        pair = jnp.where((y < 2) == (k < 2), lse[:2], lse[2:])
        pieces.append((ref, jnp.where(lax.rem(y + k, 2) == 1, pair[1:2], pair[0:1])))
    return pieces


def give_kernel(
    place, stats, rows, norms, up, down, other_up, other_down, f0, f1, f2, f3, numer_in, counts_in, left, right, held, numer, counts
):
    q = 1 - place[3]
    pieces = near_pieces(place, stats, up, down, other_up, other_down) + far_pieces(place, stats, (f0, f1, f2, f3))
    weighted(pieces, rows, norms, q, held, numer, counts, (numer_in, counts_in))
    blocks, height, width = left.shape
    for b in range(blocks):
        values, total = block_of(numer, counts, b, q, height)
        high, low = split(total)
        values = close(values, high, low).astype(BF)
        left[b] = values[:, :width]
        right[b] = values[:, width:]


def keep_kernel(
    place, stats, rows, norms, own, up, down, other_up, other_down, f0, f1, f2, f3, kept, held, numer, counts
):
    q = place[3]
    pieces = [(own, lse_of(stats, place[2]))] + near_pieces(place, stats, up, down, other_up, other_down)
    pieces += far_pieces(place, stats, (f0, f1, f2, f3))
    weighted(pieces, rows, norms, q, held, numer, counts)
    blocks, height, _ = kept.shape
    for b in range(blocks):
        values, total = block_of(numer, counts, b, q, height)
        kept[b] = close(values, total, jnp.zeros_like(total))


def merge_kernel(kept, left, right, send):
    blocks, height, width = kept.shape
    at = height - TAIL
    for b in range(blocks):
        for h, got in ((0, left), (1, right)):
            half = width // 2
            mine = kept[b, :, h * half : (h + 1) * half]
            theirs = got[b].astype(F32)
            values = mine + theirs
            tail = values[height - 8 :]
            counts = tail[8 - TAIL : 9 - TAIL, :LANES] + tail[9 - TAIL : 10 - TAIL, :LANES]
            high, low = split(counts)
            values = close(values, high, low).astype(BF)
            for c in range(half // LANES):
                send[b * N_CENT + h * (half // LANES) + c] = values[:, c * LANES : (c + 1) * LANES]


def final_kernel(got, out, scratch):
    n, height, _ = got.shape
    slot = height - TAIL
    for c in range(N_CENT):
        values = got[c].astype(F32)
        for i in range(1, n // N_CENT):
            values += got[i * N_CENT + c].astype(F32)
        tail = values[height - 8 :]
        counts = tail[8 - TAIL : 9 - TAIL] + tail[9 - TAIL : 10 - TAIL] + 1.0
        column = jnp.broadcast_to(counts, (LANES, LANES)).T
        scratch[c * slot : (c + 1) * slot] = (values / column[:height])[:slot]
    out[...] = scratch[...].astype(BF)


def body(points, centroids):
    rows, dim = centroids.shape
    pts = points.shape[0]
    n_blocks = NZ // 2
    slot = rows // (NX * NZ)
    height = slot + TAIL
    half, quarter = pts // NC, pts // NY
    x, y, core, parity = (lax.axis_index(a) for a in ("x", "y", "core", "zp"))
    place = jnp.stack([core, y, x, parity]).astype(jnp.int32)
    shape = jax.ShapeDtypeStruct

    own_half, own_quarter = pl.pallas_call(
        cut_kernel,
        out_shape=(shape((half, dim), BF), shape((quarter, dim), BF)),
        in_specs=[SMEM, VMEM],
        out_specs=(VMEM, VMEM),
        compiler_params=params(4),
        cost_estimate=CHEAP,
        name="cut",
    )(place, points)

    def ring(a, k):
        return lax.ppermute(a, "x", [(i, (i + k) % NX) for i in range(NX)])

    far = ring(own_quarter, 2)
    up, down = ring(own_half, 1), ring(own_half, NX - 1)

    points, own_half, own_quarter = lax.optimization_barrier((points, own_half, own_quarter))
    stats_shape = (NX * N_CENT, 2 * pts // LANES, LANES)
    send_stats = pl.pallas_call(
        stats_kernel,
        grid=(rows // TILE,),
        out_shape=shape(stats_shape, F32),
        in_specs=[pl.BlockSpec((pts, dim), lambda i: (0, 0)), pl.BlockSpec((TILE, dim), lambda i: (i, 0))],
        out_specs=pl.BlockSpec(stats_shape, lambda i: (0, 0, 0)),
        scratch_shapes=[pltpu.VMEM((1, pts), F32), pltpu.VMEM((1, pts), F32)],
        compiler_params=params(54),
        cost_estimate=CHEAP,
        name="stats",
    )(points, centroids)
    far, _ = lax.optimization_barrier((far, send_stats))
    stats = lax.all_to_all(send_stats, ("x", *CENT), 0, 0)
    work = n_blocks * (-(-(slot + 12) // 16) * 16)
    mine, norms = pl.pallas_call(
        window_kernel,
        out_shape=(shape((2, work, dim), BF), shape((2, work, 1), F32)),
        in_specs=[SMEM, ANY, ANY],
        out_specs=(VMEM, VMEM),
        scratch_shapes=[pltpu.SemaphoreType.DMA((NZ,))],
        compiler_params=params(50),
        cost_estimate=CHEAP,
        name="window",
    )(place, centroids, send_stats)

    def call(kernel, out_shape, n_points, *args, scratch=()):
        return pl.pallas_call(
            kernel,
            out_shape=out_shape,
            in_specs=[SMEM] + [VMEM] * (3 + len(args)),
            out_specs=jax.tree.map(lambda _: VMEM, out_shape),
            scratch_shapes=[pltpu.VMEM((n_points, dim), BF), *scratch],
            compiler_params=params(28),
            cost_estimate=CHEAP,
            name=kernel.__name__,
        )(place, stats, mine, norms, *args)

    swap = [(0, 1), (1, 0)]
    slices = [far] + [lax.ppermute(far, "y", [(i, i ^ k) for i in range(NY)]) for k in range(1, NY)]
    up, down, stats, _ = lax.optimization_barrier((up, down, stats, far))
    others = [lax.ppermute(a, "core", swap) for a in (up, down)]
    sums = (shape((work, dim), F32), shape((work, LANES), F32))
    spare = [pltpu.VMEM(s.shape, F32) for s in sums]
    numer = call(own_kernel, sums, pts, points)
    rest = (up, down, *others, *slices)
    part = shape((n_blocks, height, dim // 2), BF)
    left, right = call(give_kernel, (part, part), (NX - 1) * pts, *rest, *numer, scratch=spare)

    got_left = lax.ppermute(left, Z, [(i, i ^ 1) for i in range(NZ)])
    got_right = lax.ppermute(right, Z, [(i, (i + (1 if i % 2 else -1)) % NZ) for i in range(NZ)])
    kept = call(keep_kernel, shape((n_blocks, height, dim), F32), NX * pts, points, *rest, scratch=spare)
    send = pl.pallas_call(
        merge_kernel,
        out_shape=shape((n_blocks * N_CENT, height, LANES), BF),
        in_specs=[VMEM] * 3,
        out_specs=VMEM,
        compiler_params=params(16),
        name="merge",
    )(kept, got_left, got_right)
    got = lax.all_to_all(send, ("zq", *CENT), 0, 0)
    return pl.pallas_call(
        final_kernel,
        out_shape=shape((N_CENT * slot, LANES), BF),
        in_specs=[VMEM],
        out_specs=VMEM,
        scratch_shapes=[pltpu.VMEM((N_CENT * slot, LANES), F32)],
        compiler_params=params(16),
        name="final",
    )(got)


def solution(mesh):
    fine = Mesh(mesh.devices.reshape(NX, NZ // 2, 2, NY, NC), ("x", *Z, *CENT))
    pts = ("x", *Z)
    return jax.shard_map(
        body, mesh=fine, in_specs=(P(pts, None), P(CENT, None)), out_specs=P(pts, CENT), check_vma=False
    )
```

```python
import functools

import jax
import jax.numpy as jnp
from jax import lax
from jax.experimental import pallas as pl
from jax.experimental.pallas import tpu as pltpu
from jax.sharding import Mesh, PartitionSpec as P

BF = jnp.bfloat16
F32 = jnp.float32
NX, NZ, NY, NC = 4, 8, 4, 2
Z = ("zq", "zp")
CENT = ("y", "core")
N_CENT = NY * NC
LANES = 128
TAIL = 4
VMEM = pl.BlockSpec(memory_space=pltpu.VMEM)
SMEM = pl.BlockSpec(memory_space=pltpu.SMEM)
ANY = pl.BlockSpec(memory_space=pl.ANY)
MIB = 2**20
CHEAP = pl.CostEstimate(flops=1, bytes_accessed=1, transcendentals=0)
TILE = 640
SHIFTS = (1, NX - 1, 2)


def dot_nt(a, b):
    return lax.dot_general(a, b, (((1,), (1,)), ((), ())), preferred_element_type=F32)


def params(mib):
    return pltpu.CompilerParams(vmem_limit_bytes=mib * MIB)


def cut_kernel(place, points, half_out):
    half = half_out.shape[0]
    half_out[...] = points[pl.ds(pl.multiple_of(place[0] * half, half), half)]


def stats_kernel(points, cents, after, out, top, total):
    step = pl.program_id(0)

    @pl.when(step == 0)
    def _():
        top[...] = jnp.full_like(top, -jnp.inf)
        total[...] = jnp.zeros_like(total)

    rows = cents[...]
    chunk = rows.shape[0] // 2
    pts = points[...]
    tops, totals = [top[...]], [total[...]]
    for i in range(2):
        part = rows[i * chunk : (i + 1) * chunk]
        wide = part.astype(F32)
        logits = dot_nt(part, pts) - 0.5 * jnp.sum(wide * wide, axis=1, keepdims=True)
        high = jnp.max(logits, axis=0, keepdims=True)
        tops.append(high)
        totals.append(jnp.sum(jnp.exp(logits - high), axis=0, keepdims=True))
    new = functools.reduce(jnp.maximum, tops)
    top[...] = new
    total[...] = sum(s * jnp.exp(t - new) for s, t in zip(totals, tops))

    @pl.when(step == pl.num_programs(0) - 1)
    def _():
        groups = top.shape[1] // LANES
        both = [r[:, g * LANES : (g + 1) * LANES] for r in (top[...], total[...]) for g in range(groups)]
        out[...] = jnp.broadcast_to(jnp.concatenate(both, axis=0)[None], out.shape)


def window_kernel(place, table, after, mine, norms, sems):
    _, work, _ = mine.shape
    count = NZ // 2
    window = work // count
    stride = table.shape[0] // NX
    slot = stride // NZ
    copies = {}
    for q in range(2):
        for i in range(count):
            at = pl.multiple_of(place[2] * stride + (2 * i + q) * slot // 16 * 16, 16)
            to = mine.at[q, pl.ds(i * window, window)]
            copies[q, i] = pltpu.make_async_copy(table.at[pl.ds(at, window)], to, sems.at[q * count + i])
    for copy in copies.values():
        copy.start()
    for (q, i), copy in copies.items():
        copy.wait()
        here = slice(i * window, (i + 1) * window)
        wide = mine[q, here].astype(F32)
        norms[q, here] = 0.5 * jnp.sum(wide * wide, axis=1, keepdims=True)


def lse_of(stats, source):
    groups = stats.shape[1] // 2
    part = stats[pl.ds(source * N_CENT, N_CENT)]
    m, s = part[:, :groups], part[:, groups:]
    high = jnp.max(m, axis=0)
    return high + jnp.log(jnp.sum(s * jnp.exp(m - high[None]), axis=0))


def lse_halves(place, stats, k):
    lse = lse_of(stats, lax.rem(place[2] + NX - k, NX))
    half = lse.shape[0] // 2
    first = place[0] == 0
    return jnp.where(first, lse[:half], lse[half:]), jnp.where(first, lse[half:], lse[:half])


def weighted(pieces, rows, norms, q, held, numer, counts, before=None):
    at = 0
    lse = []
    for ref, part in pieces:
        held[at : at + ref.shape[0]] = ref[...]
        lse += [part[g : g + 1] for g in range(part.shape[0])]
        at += ref.shape[0]
    logits = dot_nt(rows[q], held[...])
    shift = norms[q]
    some = jnp.zeros(counts.shape, F32)
    weights = []
    for g, part in enumerate(lse):
        w = jnp.exp(logits[:, g * LANES : (g + 1) * LANES] - shift - part).astype(BF)
        some += w.astype(F32)
        weights.append(w)
    more = jnp.dot(jnp.concatenate(weights, axis=1), held[...], preferred_element_type=F32)
    if before is not None:
        more, some = before[0][...] + more, before[1][...] + some
    numer[...] = more
    counts[...] = some


def block_of(numer, counts, i, q, height):
    start = i * (numer.shape[0] * 2 // NZ) + 8 * (i % 2)
    found = []
    for ref in (numer, counts):
        v = ref[start : start + height]
        found.append(jnp.where(q == 1, jnp.concatenate([v[4:], v[:4]], axis=0), v))
    return found[0], row_counts(found[1])


def row_counts(part):
    part = jnp.concatenate([part, jnp.zeros((LANES - part.shape[0], LANES), F32)], axis=0)
    return jnp.sum(part.T, axis=0, keepdims=True)


def close(values, first, second):
    height, width = values.shape
    first = jnp.concatenate([first] * (width // LANES), axis=1)
    second = jnp.concatenate([second] * (width // LANES), axis=1)
    last = values[height - 8 :]
    row = lax.broadcasted_iota(jnp.int32, last.shape, 0)
    last = jnp.where(row == 8 - TAIL, first, jnp.where(row == 9 - TAIL, second, jnp.where(row > 9 - TAIL, 0.0, last)))
    return jnp.concatenate([values[: height - 8], last], axis=0)


def split(counts):
    high = counts.astype(BF).astype(F32)
    return high, counts - high


def half_pieces(place, stats, refs, which):
    return [(ref, lse_halves(place, stats, k)[which]) for k, ref in zip(SHIFTS, refs)]


def own_kernel(place, stats, rows, norms, own, numer, counts, held):
    weighted([(own, lse_of(stats, place[2]))], rows, norms, 1 - place[1], held, numer, counts)


def first_kernel(place, stats, rows, norms, up, down, far, numer_in, counts_in, numer, counts, held):
    pieces = half_pieces(place, stats, (up, down, far), 0)
    weighted(pieces, rows, norms, 1 - place[1], held, numer, counts, (numer_in, counts_in))


def give_kernel(place, stats, rows, norms, up, down, far, numer_in, counts_in, left, right, held, numer, counts):
    q = 1 - place[1]
    pieces = half_pieces(place, stats, (up, down, far), 1)
    weighted(pieces, rows, norms, q, held, numer, counts, (numer_in, counts_in))
    blocks, height, width = left.shape
    for b in range(blocks):
        values, total = block_of(numer, counts, b, q, height)
        high, low = split(total)
        values = close(values, high, low).astype(BF)
        left[b] = values[:, :width]
        right[b] = values[:, width:]


def keep_kernel(place, stats, rows, norms, own, up, down, far, up2, down2, far2, kept, held, numer, counts):
    q = place[1]
    pieces = [(own, lse_of(stats, place[2]))] + half_pieces(place, stats, (up, down, far), 0)
    pieces += half_pieces(place, stats, (up2, down2, far2), 1)
    weighted(pieces, rows, norms, q, held, numer, counts)
    blocks, height, _ = kept.shape
    for b in range(blocks):
        values, total = block_of(numer, counts, b, q, height)
        kept[b] = close(values, total, jnp.zeros_like(total))


def merge_kernel(kept, left, right, send):
    blocks, height, width = kept.shape
    at = height - TAIL
    for b in range(blocks):
        for h, got in ((0, left), (1, right)):
            half = width // 2
            mine = kept[b, :, h * half : (h + 1) * half]
            theirs = got[b].astype(F32)
            values = mine + theirs
            tail = values[height - 8 :]
            counts = tail[8 - TAIL : 9 - TAIL, :LANES] + tail[9 - TAIL : 10 - TAIL, :LANES]
            high, low = split(counts)
            values = close(values, high, low).astype(BF)
            for c in range(half // LANES):
                send[b * N_CENT + h * (half // LANES) + c] = values[:, c * LANES : (c + 1) * LANES]


def final_kernel(got, out, scratch):
    n, height, _ = got.shape
    slot = height - TAIL
    for c in range(N_CENT):
        values = got[c].astype(F32)
        for i in range(1, n // N_CENT):
            values += got[i * N_CENT + c].astype(F32)
        tail = values[height - 8 :]
        counts = tail[8 - TAIL : 9 - TAIL] + tail[9 - TAIL : 10 - TAIL] + 1.0
        column = jnp.broadcast_to(counts, (LANES, LANES)).T
        scratch[c * slot : (c + 1) * slot] = (values / column[:height])[:slot]
    out[...] = scratch[...].astype(BF)


def body(points, centroids):
    rows, dim = centroids.shape
    pts = points.shape[0]
    n_blocks = NZ // 2
    slot = rows // (NX * NZ)
    height = slot + TAIL
    half = pts // NC
    x, core, parity = (lax.axis_index(a) for a in ("x", "core", "zp"))
    place = jnp.stack([core, parity, x]).astype(jnp.int32)
    shape = jax.ShapeDtypeStruct

    own_half = pl.pallas_call(
        cut_kernel,
        out_shape=shape((half, dim), BF),
        in_specs=[SMEM, VMEM],
        out_specs=VMEM,
        compiler_params=params(4),
        cost_estimate=CHEAP,
        name="cut",
    )(place, points)
    near = [lax.ppermute(own_half, "x", [(i, (i + k) % NX) for i in range(NX)]) for k in SHIFTS]

    stats_shape = (NX * N_CENT, 2 * pts // LANES, LANES)
    send_stats = pl.pallas_call(
        stats_kernel,
        grid=(rows // TILE,),
        out_shape=shape(stats_shape, F32),
        in_specs=[pl.BlockSpec((pts, dim), lambda i: (0, 0)), pl.BlockSpec((TILE, dim), lambda i: (i, 0)), ANY],
        out_specs=pl.BlockSpec(stats_shape, lambda i: (0, 0, 0)),
        scratch_shapes=[pltpu.VMEM((1, pts), F32), pltpu.VMEM((1, pts), F32)],
        compiler_params=params(54),
        cost_estimate=CHEAP,
        name="stats",
    )(points, centroids, own_half)
    stats = lax.all_to_all(send_stats, ("x", *CENT), 0, 0)
    work = n_blocks * (-(-(slot + 12) // 16) * 16)
    mine, norms = pl.pallas_call(
        window_kernel,
        out_shape=(shape((2, work, dim), BF), shape((2, work, 1), F32)),
        in_specs=[SMEM, ANY, ANY],
        out_specs=(VMEM, VMEM),
        scratch_shapes=[pltpu.SemaphoreType.DMA((NZ,))],
        compiler_params=params(50),
        cost_estimate=CHEAP,
        name="window",
    )(place, centroids, send_stats)

    def call(kernel, out_shape, n_points, *args, scratch=()):
        return pl.pallas_call(
            kernel,
            out_shape=out_shape,
            in_specs=[SMEM] + [VMEM] * (3 + len(args)),
            out_specs=jax.tree.map(lambda _: VMEM, out_shape),
            scratch_shapes=[pltpu.VMEM((n_points, dim), BF), *scratch],
            compiler_params=params(28),
            cost_estimate=CHEAP,
            name=kernel.__name__,
        )(place, stats, mine, norms, *args)

    sums = (shape((work, dim), F32), shape((work, LANES), F32))
    spare = [pltpu.VMEM(s.shape, F32) for s in sums]
    numer = call(own_kernel, sums, pts, points)
    near, numer = lax.optimization_barrier((near, numer))
    others = [lax.ppermute(a, "core", [(0, 1), (1, 0)]) for a in near]
    numer = call(first_kernel, sums, 3 * half, *near, *numer)
    others, numer = lax.optimization_barrier((others, numer))
    part = shape((n_blocks, height, dim // 2), BF)
    left, right = call(give_kernel, (part, part), 3 * half, *others, *numer, scratch=spare)

    got_left = lax.ppermute(left, Z, [(i, i ^ 1) for i in range(NZ)])
    got_right = lax.ppermute(right, Z, [(i, (i + (1 if i % 2 else -1)) % NZ) for i in range(NZ)])
    kept = call(keep_kernel, shape((n_blocks, height, dim), F32), NX * pts, points, *near, *others, scratch=spare)
    send = pl.pallas_call(
        merge_kernel,
        out_shape=shape((n_blocks * N_CENT, height, LANES), BF),
        in_specs=[VMEM] * 3,
        out_specs=VMEM,
        compiler_params=params(16),
        name="merge",
    )(kept, got_left, got_right)
    got = lax.all_to_all(send, ("zq", *CENT), 0, 0)
    return pl.pallas_call(
        final_kernel,
        out_shape=shape((N_CENT * slot, LANES), BF),
        in_specs=[VMEM],
        out_specs=VMEM,
        scratch_shapes=[pltpu.VMEM((N_CENT * slot, LANES), F32)],
        compiler_params=params(16),
        name="final",
    )(got)


def solution(mesh):
    fine = Mesh(mesh.devices.reshape(NX, NZ // 2, 2, NY, NC), ("x", *Z, *CENT))
    pts = ("x", *Z)
    return jax.shard_map(
        body, mesh=fine, in_specs=(P(pts, None), P(CENT, None)), out_specs=P(pts, CENT), check_vma=False
    )
```

```python
import functools

import jax
import jax.numpy as jnp
from jax import lax
from jax.experimental import pallas as pl
from jax.experimental.pallas import tpu as pltpu
from jax.sharding import Mesh, PartitionSpec as P

BF = jnp.bfloat16
F32 = jnp.float32
NX, NZ, NY, NC = 4, 8, 4, 2
Z = ("zq", "zp")
CENT = ("y", "core")
N_CENT = NY * NC
LANES = 128
TAIL = 4
VMEM = pl.BlockSpec(memory_space=pltpu.VMEM)
SMEM = pl.BlockSpec(memory_space=pltpu.SMEM)
ANY = pl.BlockSpec(memory_space=pl.ANY)
MIB = 2**20
CHEAP = pl.CostEstimate(flops=1, bytes_accessed=1, transcendentals=0)
TILE = 640
LEFT = 640
SHIFTS = (1, NX - 1, 2)


def dot_nt(a, b):
    return lax.dot_general(a, b, (((1,), (1,)), ((), ())), preferred_element_type=F32)


def params(mib):
    return pltpu.CompilerParams(vmem_limit_bytes=mib * MIB)


def cut_kernel(place, points, half_out):
    half = half_out.shape[0]
    half_out[...] = points[pl.ds(pl.multiple_of(place[0] * half, half), half)]


def stats_kernel(points, cents, after, out, top, total):
    step = pl.program_id(0)

    @pl.when(step == 0)
    def _():
        top[...] = jnp.full_like(top, -jnp.inf)
        total[...] = jnp.zeros_like(total)

    rows = cents[...]
    chunk = rows.shape[0] // 2
    pts = points[...]
    tops, totals = [top[...]], [total[...]]
    for i in range(2):
        part = rows[i * chunk : (i + 1) * chunk]
        wide = part.astype(F32)
        logits = dot_nt(part, pts) - 0.5 * jnp.sum(wide * wide, axis=1, keepdims=True)
        high = jnp.max(logits, axis=0, keepdims=True)
        tops.append(high)
        totals.append(jnp.sum(jnp.exp(logits - high), axis=0, keepdims=True))
    new = functools.reduce(jnp.maximum, tops)
    top[...] = new
    total[...] = sum(s * jnp.exp(t - new) for s, t in zip(totals, tops))

    @pl.when(step == pl.num_programs(0) - 1)
    def _():
        groups = top.shape[1] // LANES
        both = [r[:, g * LANES : (g + 1) * LANES] for r in (top[...], total[...]) for g in range(groups)]
        out[...] = jnp.broadcast_to(jnp.concatenate(both, axis=0)[None], out.shape)


def window_kernel(place, table, after, mine, norms, sems):
    _, work, _ = mine.shape
    count = NZ // 2
    window = work // count
    stride = table.shape[0] // NX
    slot = stride // NZ
    copies = {}
    for q in range(2):
        for i in range(count):
            at = pl.multiple_of(place[2] * stride + (2 * i + q) * slot // 16 * 16, 16)
            to = mine.at[q, pl.ds(i * window, window)]
            copies[q, i] = pltpu.make_async_copy(table.at[pl.ds(at, window)], to, sems.at[q * count + i])
    for copy in copies.values():
        copy.start()
    for (q, i), copy in copies.items():
        copy.wait()
        here = slice(i * window, (i + 1) * window)
        wide = mine[q, here].astype(F32)
        norms[q, here] = 0.5 * jnp.sum(wide * wide, axis=1, keepdims=True)


def lse_of(stats, source):
    groups = stats.shape[1] // 2
    part = stats[pl.ds(source * N_CENT, N_CENT)]
    m, s = part[:, :groups], part[:, groups:]
    high = jnp.max(m, axis=0)
    return high + jnp.log(jnp.sum(s * jnp.exp(m - high[None]), axis=0))


def lse_halves(place, stats, k):
    lse = lse_of(stats, lax.rem(place[2] + NX - k, NX))
    half = lse.shape[0] // 2
    first = place[0] == 0
    return jnp.where(first, lse[:half], lse[half:]), jnp.where(first, lse[half:], lse[:half])


def weighted(pieces, rows, norms, q, held, numer, counts, before=None):
    at = 0
    lse = []
    for ref, part in pieces:
        held[at : at + ref.shape[0]] = ref[...]
        lse += [part[g : g + 1] for g in range(part.shape[0])]
        at += ref.shape[0]
    logits = dot_nt(rows[q], held[...])
    shift = norms[q]
    some = jnp.zeros(counts.shape, F32)
    weights = []
    for g, part in enumerate(lse):
        w = jnp.exp(logits[:, g * LANES : (g + 1) * LANES] - shift - part).astype(BF)
        some += w.astype(F32)
        weights.append(w)
    more = jnp.dot(jnp.concatenate(weights, axis=1), held[...], preferred_element_type=F32)
    if before is not None:
        more, some = before[0][...] + more, before[1][...] + some
    numer[...] = more
    counts[...] = some


def block_of(numer, counts, i, q, height):
    start = i * (numer.shape[0] * 2 // NZ) + 8 * (i % 2)
    found = []
    for ref in (numer, counts):
        v = ref[start : start + height]
        found.append(jnp.where(q == 1, jnp.concatenate([v[4:], v[:4]], axis=0), v))
    return found[0], row_counts(found[1])


def row_counts(part):
    part = jnp.concatenate([part, jnp.zeros((LANES - part.shape[0], LANES), F32)], axis=0)
    return jnp.sum(part.T, axis=0, keepdims=True)


def close(values, first, second):
    height, width = values.shape
    first = jnp.concatenate([first] * (width // LANES), axis=1)
    second = jnp.concatenate([second] * (width // LANES), axis=1)
    last = values[height - 8 :]
    row = lax.broadcasted_iota(jnp.int32, last.shape, 0)
    last = jnp.where(row == 8 - TAIL, first, jnp.where(row == 9 - TAIL, second, jnp.where(row > 9 - TAIL, 0.0, last)))
    return jnp.concatenate([values[: height - 8], last], axis=0)


def split(counts):
    high = counts.astype(BF).astype(F32)
    return high, counts - high


def half_pieces(place, stats, refs, which):
    return [(ref, lse_halves(place, stats, k)[which]) for k, ref in zip(SHIFTS, refs)]


def first_kernel(place, stats, rows, norms, own, up, down, far, numer, counts, held):
    pieces = [(own, lse_of(stats, place[2]))] + half_pieces(place, stats, (up, down, far), 0)
    weighted(pieces, rows, norms, 1 - place[1], held, numer, counts)


def give_kernel(place, stats, rows, norms, up, down, far, numer_in, counts_in, left, right, held, numer, counts):
    q = 1 - place[1]
    pieces = half_pieces(place, stats, (up, down, far), 1)
    weighted(pieces, rows, norms, q, held, numer, counts, (numer_in, counts_in))
    blocks, height, width = left.shape
    for b in range(blocks):
        values, total = block_of(numer, counts, b, q, height)
        high, low = split(total)
        values = close(values, high, low).astype(BF)
        left[b] = values[:, :width]
        right[b] = values[:, width:]


def keep_kernel(place, stats, rows, norms, own, up, down, far, up2, down2, far2, kept, held, numer, counts):
    q = place[1]
    pieces = [(own, lse_of(stats, place[2]))] + half_pieces(place, stats, (up, down, far), 0)
    pieces += half_pieces(place, stats, (up2, down2, far2), 1)
    weighted(pieces, rows, norms, q, held, numer, counts)
    blocks, height, _ = kept.shape
    for b in range(blocks):
        values, total = block_of(numer, counts, b, q, height)
        kept[b] = close(values, total, jnp.zeros_like(total))


def merge_kernel(kept, left, right, send):
    blocks, height, _ = kept.shape
    for b in range(blocks):
        at = 0
        for got in (left, right):
            width = got.shape[2]
            values = kept[b, :, at : at + width] + got[b].astype(F32)
            tail = values[height - 8 :]
            counts = tail[8 - TAIL : 9 - TAIL, :LANES] + tail[9 - TAIL : 10 - TAIL, :LANES]
            high, low = split(counts)
            values = close(values, high, low).astype(BF)
            for c in range(width // LANES):
                send[b * N_CENT + at // LANES + c] = values[:, c * LANES : (c + 1) * LANES]
            at += width


def final_kernel(got, out, scratch):
    n, height, _ = got.shape
    slot = height - TAIL
    for c in range(N_CENT):
        values = got[c].astype(F32)
        for i in range(1, n // N_CENT):
            values += got[i * N_CENT + c].astype(F32)
        tail = values[height - 8 :]
        counts = tail[8 - TAIL : 9 - TAIL] + tail[9 - TAIL : 10 - TAIL] + 1.0
        column = jnp.broadcast_to(counts, (LANES, LANES)).T
        scratch[c * slot : (c + 1) * slot] = (values / column[:height])[:slot]
    out[...] = scratch[...].astype(BF)


def body(points, centroids):
    rows, dim = centroids.shape
    pts = points.shape[0]
    n_blocks = NZ // 2
    slot = rows // (NX * NZ)
    height = slot + TAIL
    half = pts // NC
    x, core, parity = (lax.axis_index(a) for a in ("x", "core", "zp"))
    place = jnp.stack([core, parity, x]).astype(jnp.int32)
    shape = jax.ShapeDtypeStruct

    own_half = pl.pallas_call(
        cut_kernel,
        out_shape=shape((half, dim), BF),
        in_specs=[SMEM, VMEM],
        out_specs=VMEM,
        compiler_params=params(4),
        cost_estimate=CHEAP,
        name="cut",
    )(place, points)
    near = [lax.ppermute(own_half, "x", [(i, (i + k) % NX) for i in range(NX)]) for k in SHIFTS]

    stats_shape = (NX * N_CENT, 2 * pts // LANES, LANES)
    send_stats = pl.pallas_call(
        stats_kernel,
        grid=(rows // TILE,),
        out_shape=shape(stats_shape, F32),
        in_specs=[pl.BlockSpec((pts, dim), lambda i: (0, 0)), pl.BlockSpec((TILE, dim), lambda i: (i, 0)), ANY],
        out_specs=pl.BlockSpec(stats_shape, lambda i: (0, 0, 0)),
        scratch_shapes=[pltpu.VMEM((1, pts), F32), pltpu.VMEM((1, pts), F32)],
        compiler_params=params(54),
        cost_estimate=CHEAP,
        name="stats",
    )(points, centroids, own_half)
    stats = lax.all_to_all(send_stats, ("x", *CENT), 0, 0)
    work = n_blocks * (-(-(slot + 12) // 16) * 16)
    mine, norms = pl.pallas_call(
        window_kernel,
        out_shape=(shape((2, work, dim), BF), shape((2, work, 1), F32)),
        in_specs=[SMEM, ANY, ANY],
        out_specs=(VMEM, VMEM),
        scratch_shapes=[pltpu.SemaphoreType.DMA((NZ,))],
        compiler_params=params(50),
        cost_estimate=CHEAP,
        name="window",
    )(place, centroids, send_stats)

    def call(kernel, out_shape, n_points, *args, scratch=()):
        return pl.pallas_call(
            kernel,
            out_shape=out_shape,
            in_specs=[SMEM] + [VMEM] * (3 + len(args)),
            out_specs=jax.tree.map(lambda _: VMEM, out_shape),
            scratch_shapes=[pltpu.VMEM((n_points, dim), BF), *scratch],
            compiler_params=params(28),
            cost_estimate=CHEAP,
            name=kernel.__name__,
        )(place, stats, mine, norms, *args)

    sums = (shape((work, dim), F32), shape((work, LANES), F32))
    spare = [pltpu.VMEM(s.shape, F32) for s in sums]
    near, stats = lax.optimization_barrier((near, stats))
    others = [lax.ppermute(a, "core", [(0, 1), (1, 0)]) for a in near]
    numer = call(first_kernel, sums, pts + 3 * half, points, *near)
    others, numer = lax.optimization_barrier((others, numer))
    parts = tuple(shape((n_blocks, height, width), BF) for width in (LEFT, dim - LEFT))
    left, right = call(give_kernel, parts, 3 * half, *others, *numer, scratch=spare)

    got_left = lax.ppermute(left, Z, [(i, i ^ 1) for i in range(NZ)])
    got_right = lax.ppermute(right, Z, [(i, (i + (1 if i % 2 else -1)) % NZ) for i in range(NZ)])
    kept = call(keep_kernel, shape((n_blocks, height, dim), F32), NX * pts, points, *near, *others, scratch=spare)
    send = pl.pallas_call(
        merge_kernel,
        out_shape=shape((n_blocks * N_CENT, height, LANES), BF),
        in_specs=[VMEM] * 3,
        out_specs=VMEM,
        compiler_params=params(16),
        name="merge",
    )(kept, got_left, got_right)
    got = lax.all_to_all(send, ("zq", *CENT), 0, 0)
    return pl.pallas_call(
        final_kernel,
        out_shape=shape((N_CENT * slot, LANES), BF),
        in_specs=[VMEM],
        out_specs=VMEM,
        scratch_shapes=[pltpu.VMEM((N_CENT * slot, LANES), F32)],
        compiler_params=params(16),
        name="final",
    )(got)


def solution(mesh):
    fine = Mesh(mesh.devices.reshape(NX, NZ // 2, 2, NY, NC), ("x", *Z, *CENT))
    pts = ("x", *Z)
    return jax.shard_map(
        body, mesh=fine, in_specs=(P(pts, None), P(CENT, None)), out_specs=P(pts, CENT), check_vma=False
    )
```

```python
import functools

import jax
import jax.numpy as jnp
from jax import lax
from jax.experimental import pallas as pl
from jax.experimental.pallas import tpu as pltpu
from jax.sharding import Mesh, PartitionSpec as P

BF = jnp.bfloat16
F32 = jnp.float32
NX, NZ, NY, NC = 4, 8, 4, 2
Z = ("zq", "zp")
CENT = ("y", "core")
N_CENT = NY * NC
LANES = 128
TAIL = 4
VMEM = pl.BlockSpec(memory_space=pltpu.VMEM)
SMEM = pl.BlockSpec(memory_space=pltpu.SMEM)
ANY = pl.BlockSpec(memory_space=pl.ANY)
MIB = 2**20
CHEAP = pl.CostEstimate(flops=1, bytes_accessed=1, transcendentals=0)
TILE = 640
LEFT = 640
SHIFTS = (1, NX - 1, 2)


def dot_nt(a, b):
    return lax.dot_general(a, b, (((1,), (1,)), ((), ())), preferred_element_type=F32)


def params(mib):
    return pltpu.CompilerParams(vmem_limit_bytes=mib * MIB)


def cut_kernel(place, points, half_out):
    half = half_out.shape[0]
    half_out[...] = points[pl.ds(pl.multiple_of(place[0] * half, half), half)]


def stats_kernel(points, cents, after, out, flag, top, total):
    step = pl.program_id(0)

    @pl.when(step == 0)
    def _():
        top[...] = jnp.full_like(top, -jnp.inf)
        total[...] = jnp.zeros_like(total)

    rows = cents[...]
    chunk = rows.shape[0] // 2
    pts = points[...]
    tops, totals = [top[...]], [total[...]]
    for i in range(2):
        part = rows[i * chunk : (i + 1) * chunk]
        wide = part.astype(F32)
        logits = dot_nt(part, pts) - 0.5 * jnp.sum(wide * wide, axis=1, keepdims=True)
        high = jnp.max(logits, axis=0, keepdims=True)
        tops.append(high)
        totals.append(jnp.sum(jnp.exp(logits - high), axis=0, keepdims=True))
    new = functools.reduce(jnp.maximum, tops)
    top[...] = new
    total[...] = sum(s * jnp.exp(t - new) for s, t in zip(totals, tops))

    @pl.when(step == pl.num_programs(0) - 1)
    def _():
        groups = top.shape[1] // LANES
        both = [r[:, g * LANES : (g + 1) * LANES] for r in (top[...], total[...]) for g in range(groups)]
        out[...] = jnp.broadcast_to(jnp.concatenate(both, axis=0)[None], out.shape)
        flag[...] = jnp.zeros_like(flag)


def window_kernel(place, table, after, mine, norms, sems):
    _, work, _ = mine.shape
    count = NZ // 2
    window = work // count
    stride = table.shape[0] // NX
    slot = stride // NZ
    copies = {}
    for q in range(2):
        for i in range(count):
            at = pl.multiple_of(place[2] * stride + (2 * i + q) * slot // 16 * 16, 16)
            to = mine.at[q, pl.ds(i * window, window)]
            copies[q, i] = pltpu.make_async_copy(table.at[pl.ds(at, window)], to, sems.at[q * count + i])
    for copy in copies.values():
        copy.start()
    for (q, i), copy in copies.items():
        copy.wait()
        here = slice(i * window, (i + 1) * window)
        wide = mine[q, here].astype(F32)
        norms[q, here] = 0.5 * jnp.sum(wide * wide, axis=1, keepdims=True)


def lse_of(stats, source):
    groups = stats.shape[1] // 2
    part = stats[pl.ds(source * N_CENT, N_CENT)]
    m, s = part[:, :groups], part[:, groups:]
    high = jnp.max(m, axis=0)
    return high + jnp.log(jnp.sum(s * jnp.exp(m - high[None]), axis=0))


def lse_halves(place, stats, k):
    lse = lse_of(stats, lax.rem(place[2] + NX - k, NX))
    half = lse.shape[0] // 2
    first = place[0] == 0
    return jnp.where(first, lse[:half], lse[half:]), jnp.where(first, lse[half:], lse[:half])


def weighted(pieces, rows, norms, q, held, numer, counts, before=None):
    at = 0
    lse = []
    for ref, part in pieces:
        held[at : at + ref.shape[0]] = ref[...]
        lse += [part[g : g + 1] for g in range(part.shape[0])]
        at += ref.shape[0]
    logits = dot_nt(rows[q], held[...])
    shift = norms[q]
    some = jnp.zeros(counts.shape, F32)
    weights = []
    for g, part in enumerate(lse):
        w = jnp.exp(logits[:, g * LANES : (g + 1) * LANES] - shift - part).astype(BF)
        some += w.astype(F32)
        weights.append(w)
    more = jnp.dot(jnp.concatenate(weights, axis=1), held[...], preferred_element_type=F32)
    if before is not None:
        more, some = before[0][...] + more, before[1][...] + some
    numer[...] = more
    counts[...] = some


def block_of(numer, counts, i, q, height):
    start = i * (numer.shape[0] * 2 // NZ) + 8 * (i % 2)
    found = []
    for ref in (numer, counts):
        v = ref[start : start + height]
        found.append(jnp.where(q == 1, jnp.concatenate([v[4:], v[:4]], axis=0), v))
    return found[0], row_counts(found[1])


def row_counts(part):
    part = jnp.concatenate([part, jnp.zeros((LANES - part.shape[0], LANES), F32)], axis=0)
    return jnp.sum(part.T, axis=0, keepdims=True)


def close(values, first, second):
    height, width = values.shape
    first = jnp.concatenate([first] * (width // LANES), axis=1)
    second = jnp.concatenate([second] * (width // LANES), axis=1)
    last = values[height - 8 :]
    row = lax.broadcasted_iota(jnp.int32, last.shape, 0)
    last = jnp.where(row == 8 - TAIL, first, jnp.where(row == 9 - TAIL, second, jnp.where(row > 9 - TAIL, 0.0, last)))
    return jnp.concatenate([values[: height - 8], last], axis=0)


def split(counts):
    high = counts.astype(BF).astype(F32)
    return high, counts - high


def half_pieces(place, stats, refs, which):
    return [(ref, lse_halves(place, stats, k)[which]) for k, ref in zip(SHIFTS, refs)]


def first_kernel(place, stats, rows, norms, own, up, down, far, numer, counts, held):
    pieces = [(own, lse_of(stats, place[2]))] + half_pieces(place, stats, (up, down, far), 0)
    weighted(pieces, rows, norms, 1 - place[1], held, numer, counts)


def give_kernel(place, stats, rows, norms, up, down, far, numer_in, counts_in, left, right, held, numer, counts):
    q = 1 - place[1]
    pieces = half_pieces(place, stats, (up, down, far), 1)
    weighted(pieces, rows, norms, q, held, numer, counts, (numer_in, counts_in))
    blocks, height, width = left.shape
    for b in range(blocks):
        values, total = block_of(numer, counts, b, q, height)
        high, low = split(total)
        values = close(values, high, low).astype(BF)
        left[b] = values[:, :width]
        right[b] = values[:, width:]


def keep_kernel(place, stats, rows, norms, own, up, down, far, up2, down2, far2, kept, held, numer, counts):
    q = place[1]
    pieces = [(own, lse_of(stats, place[2]))] + half_pieces(place, stats, (up, down, far), 0)
    pieces += half_pieces(place, stats, (up2, down2, far2), 1)
    weighted(pieces, rows, norms, q, held, numer, counts)
    blocks, height, _ = kept.shape
    for b in range(blocks):
        values, total = block_of(numer, counts, b, q, height)
        kept[b] = close(values, total, jnp.zeros_like(total))


def merge_kernel(kept, left, right, send):
    blocks, height, _ = kept.shape
    for b in range(blocks):
        at = 0
        for got in (left, right):
            width = got.shape[2]
            values = kept[b, :, at : at + width] + got[b].astype(F32)
            tail = values[height - 8 :]
            counts = tail[8 - TAIL : 9 - TAIL, :LANES] + tail[9 - TAIL : 10 - TAIL, :LANES]
            high, low = split(counts)
            values = close(values, high, low).astype(BF)
            for c in range(width // LANES):
                send[b * N_CENT + at // LANES + c] = values[:, c * LANES : (c + 1) * LANES]
            at += width


def final_kernel(got, out, scratch):
    n, height, _ = got.shape
    slot = height - TAIL
    for c in range(N_CENT):
        values = got[c].astype(F32)
        for i in range(1, n // N_CENT):
            values += got[i * N_CENT + c].astype(F32)
        tail = values[height - 8 :]
        counts = tail[8 - TAIL : 9 - TAIL] + tail[9 - TAIL : 10 - TAIL] + 1.0
        column = jnp.broadcast_to(counts, (LANES, LANES)).T
        scratch[c * slot : (c + 1) * slot] = (values / column[:height])[:slot]
    out[...] = scratch[...].astype(BF)


def body(points, centroids):
    rows, dim = centroids.shape
    pts = points.shape[0]
    n_blocks = NZ // 2
    slot = rows // (NX * NZ)
    height = slot + TAIL
    half = pts // NC
    x, core, parity = (lax.axis_index(a) for a in ("x", "core", "zp"))
    place = jnp.stack([core, parity, x]).astype(jnp.int32)
    shape = jax.ShapeDtypeStruct

    own_half = pl.pallas_call(
        cut_kernel,
        out_shape=shape((half, dim), BF),
        in_specs=[SMEM, VMEM],
        out_specs=VMEM,
        compiler_params=params(4),
        cost_estimate=CHEAP,
        name="cut",
    )(place, points)
    near = [lax.ppermute(own_half, "x", [(i, (i + k) % NX) for i in range(NX)]) for k in SHIFTS]

    stats_shape = (NX * N_CENT, 2 * pts // LANES, LANES)
    send_stats, flag = pl.pallas_call(
        stats_kernel,
        grid=(rows // TILE,),
        out_shape=(shape(stats_shape, F32), shape((8, LANES), F32)),
        in_specs=[pl.BlockSpec((pts, dim), lambda i: (0, 0)), pl.BlockSpec((TILE, dim), lambda i: (i, 0)), ANY],
        out_specs=(pl.BlockSpec(stats_shape, lambda i: (0, 0, 0)), pl.BlockSpec((8, LANES), lambda i: (0, 0))),
        scratch_shapes=[pltpu.VMEM((1, pts), F32), pltpu.VMEM((1, pts), F32)],
        compiler_params=params(54),
        cost_estimate=CHEAP,
        name="stats",
    )(points, centroids, own_half)
    stats = lax.all_to_all(send_stats, ("x", *CENT), 0, 0)
    work = n_blocks * (-(-(slot + 12) // 16) * 16)
    mine, norms = pl.pallas_call(
        window_kernel,
        out_shape=(shape((2, work, dim), BF), shape((2, work, 1), F32)),
        in_specs=[SMEM, ANY, ANY],
        out_specs=(VMEM, VMEM),
        scratch_shapes=[pltpu.SemaphoreType.DMA((NZ,))],
        compiler_params=params(50),
        cost_estimate=CHEAP,
        name="window",
    )(place, centroids, flag)

    def call(kernel, out_shape, n_points, *args, scratch=()):
        return pl.pallas_call(
            kernel,
            out_shape=out_shape,
            in_specs=[SMEM] + [VMEM] * (3 + len(args)),
            out_specs=jax.tree.map(lambda _: VMEM, out_shape),
            scratch_shapes=[pltpu.VMEM((n_points, dim), BF), *scratch],
            compiler_params=params(28),
            cost_estimate=CHEAP,
            name=kernel.__name__,
        )(place, stats, mine, norms, *args)

    sums = (shape((work, dim), F32), shape((work, LANES), F32))
    spare = [pltpu.VMEM(s.shape, F32) for s in sums]
    near, stats, mine, norms = lax.optimization_barrier((near, stats, mine, norms))
    others = [lax.ppermute(a, "core", [(0, 1), (1, 0)]) for a in near]
    numer = call(first_kernel, sums, pts + 3 * half, points, *near)
    others, numer = lax.optimization_barrier((others, numer))
    parts = tuple(shape((n_blocks, height, width), BF) for width in (LEFT, dim - LEFT))
    left, right = call(give_kernel, parts, 3 * half, *others, *numer, scratch=spare)

    got_left = lax.ppermute(left, Z, [(i, i ^ 1) for i in range(NZ)])
    got_right = lax.ppermute(right, Z, [(i, (i + (1 if i % 2 else -1)) % NZ) for i in range(NZ)])
    kept = call(keep_kernel, shape((n_blocks, height, dim), F32), NX * pts, points, *near, *others, scratch=spare)
    send = pl.pallas_call(
        merge_kernel,
        out_shape=shape((n_blocks * N_CENT, height, LANES), BF),
        in_specs=[VMEM] * 3,
        out_specs=VMEM,
        compiler_params=params(16),
        name="merge",
    )(kept, got_left, got_right)
    got = lax.all_to_all(send, ("zq", *CENT), 0, 0)
    return pl.pallas_call(
        final_kernel,
        out_shape=shape((N_CENT * slot, LANES), BF),
        in_specs=[VMEM],
        out_specs=VMEM,
        scratch_shapes=[pltpu.VMEM((N_CENT * slot, LANES), F32)],
        compiler_params=params(16),
        name="final",
    )(got)


def solution(mesh):
    fine = Mesh(mesh.devices.reshape(NX, NZ // 2, 2, NY, NC), ("x", *Z, *CENT))
    pts = ("x", *Z)
    return jax.shard_map(
        body, mesh=fine, in_specs=(P(pts, None), P(CENT, None)), out_specs=P(pts, CENT), check_vma=False
    )
```

```python
import functools

import jax
import jax.numpy as jnp
from jax import lax
from jax.experimental import pallas as pl
from jax.experimental.pallas import tpu as pltpu
from jax.sharding import Mesh, PartitionSpec as P

BF = jnp.bfloat16
F32 = jnp.float32
NX, NZ, NY, NC = 4, 8, 4, 2
Z = ("zq", "zp")
CENT = ("y", "core")
N_CENT = NY * NC
LANES = 128
TAIL = 4
VMEM = pl.BlockSpec(memory_space=pltpu.VMEM)
SMEM = pl.BlockSpec(memory_space=pltpu.SMEM)
ANY = pl.BlockSpec(memory_space=pl.ANY)
MIB = 2**20
CHEAP = pl.CostEstimate(flops=1, bytes_accessed=1, transcendentals=0)
CHUNKS = 5
LEFT = 640
SHIFTS = (1, NX - 1, 2)


def dot_nt(a, b):
    return lax.dot_general(a, b, (((1,), (1,)), ((), ())), preferred_element_type=F32)


def params(mib):
    return pltpu.CompilerParams(vmem_limit_bytes=mib * MIB)


def cut_kernel(place, points, cents, half_out):
    half = half_out.shape[0]
    half_out[...] = points[pl.ds(pl.multiple_of(place[0] * half, half), half)]


def stats_kernel(points, cents, after, out, flag):
    chunk = cents.shape[0] // CHUNKS
    pts = points[...]
    tops, totals = [], []
    for i in range(CHUNKS):
        rows = cents[i * chunk : (i + 1) * chunk]
        wide = rows.astype(F32)
        logits = dot_nt(rows, pts) - 0.5 * jnp.sum(wide * wide, axis=1, keepdims=True)
        top = jnp.max(logits, axis=0, keepdims=True)
        tops.append(top)
        totals.append(jnp.sum(jnp.exp(logits - top), axis=0, keepdims=True))
    top = functools.reduce(jnp.maximum, tops)
    total = sum(s * jnp.exp(t - top) for s, t in zip(totals, tops))
    groups = top.shape[1] // LANES
    both = [r[:, g * LANES : (g + 1) * LANES] for r in (top, total) for g in range(groups)]
    out[...] = jnp.broadcast_to(jnp.concatenate(both, axis=0)[None], out.shape)
    flag[...] = jnp.zeros_like(flag)


def window_kernel(place, table, after, mine, norms, sems):
    _, work, _ = mine.shape
    count = NZ // 2
    window = work // count
    stride = table.shape[0] // NX
    slot = stride // NZ
    copies = {}
    for q in range(2):
        for i in range(count):
            at = pl.multiple_of(place[2] * stride + (2 * i + q) * slot // 16 * 16, 16)
            to = mine.at[q, pl.ds(i * window, window)]
            copies[q, i] = pltpu.make_async_copy(table.at[pl.ds(at, window)], to, sems.at[q * count + i])
    for copy in copies.values():
        copy.start()
    for (q, i), copy in copies.items():
        copy.wait()
        here = slice(i * window, (i + 1) * window)
        wide = mine[q, here].astype(F32)
        norms[q, here] = 0.5 * jnp.sum(wide * wide, axis=1, keepdims=True)


def lse_of(stats, source):
    groups = stats.shape[1] // 2
    part = stats[pl.ds(source * N_CENT, N_CENT)]
    m, s = part[:, :groups], part[:, groups:]
    high = jnp.max(m, axis=0)
    return high + jnp.log(jnp.sum(s * jnp.exp(m - high[None]), axis=0))


def lse_halves(place, stats, k):
    lse = lse_of(stats, lax.rem(place[2] + NX - k, NX))
    half = lse.shape[0] // 2
    first = place[0] == 0
    return jnp.where(first, lse[:half], lse[half:]), jnp.where(first, lse[half:], lse[:half])


def weighted(pieces, rows, norms, q, held, numer, counts, before=None):
    at = 0
    lse = []
    for ref, part in pieces:
        held[at : at + ref.shape[0]] = ref[...]
        lse += [part[g : g + 1] for g in range(part.shape[0])]
        at += ref.shape[0]
    logits = dot_nt(rows[q], held[...])
    shift = norms[q]
    some = jnp.zeros(counts.shape, F32)
    weights = []
    for g, part in enumerate(lse):
        w = jnp.exp(logits[:, g * LANES : (g + 1) * LANES] - shift - part).astype(BF)
        some += w.astype(F32)
        weights.append(w)
    more = jnp.dot(jnp.concatenate(weights, axis=1), held[...], preferred_element_type=F32)
    if before is not None:
        more, some = before[0][...] + more, before[1][...] + some
    numer[...] = more
    counts[...] = some


def block_of(numer, counts, i, q, height):
    start = i * (numer.shape[0] * 2 // NZ) + 8 * (i % 2)
    found = []
    for ref in (numer, counts):
        v = ref[start : start + height]
        found.append(jnp.where(q == 1, jnp.concatenate([v[4:], v[:4]], axis=0), v))
    return found[0], row_counts(found[1])


def row_counts(part):
    part = jnp.concatenate([part, jnp.zeros((LANES - part.shape[0], LANES), F32)], axis=0)
    return jnp.sum(part.T, axis=0, keepdims=True)


def close(values, first, second):
    height, width = values.shape
    first = jnp.concatenate([first] * (width // LANES), axis=1)
    second = jnp.concatenate([second] * (width // LANES), axis=1)
    last = values[height - 8 :]
    row = lax.broadcasted_iota(jnp.int32, last.shape, 0)
    last = jnp.where(row == 8 - TAIL, first, jnp.where(row == 9 - TAIL, second, jnp.where(row > 9 - TAIL, 0.0, last)))
    return jnp.concatenate([values[: height - 8], last], axis=0)


def split(counts):
    high = counts.astype(BF).astype(F32)
    return high, counts - high


def half_pieces(place, stats, refs, which):
    return [(ref, lse_halves(place, stats, k)[which]) for k, ref in zip(SHIFTS, refs)]


def first_kernel(place, stats, rows, norms, own, up, down, far, numer, counts, held):
    pieces = [(own, lse_of(stats, place[2]))] + half_pieces(place, stats, (up, down, far), 0)
    weighted(pieces, rows, norms, 1 - place[1], held, numer, counts)


def give_kernel(place, stats, rows, norms, up, down, far, numer_in, counts_in, left, right, held, numer, counts):
    q = 1 - place[1]
    pieces = half_pieces(place, stats, (up, down, far), 1)
    weighted(pieces, rows, norms, q, held, numer, counts, (numer_in, counts_in))
    blocks, height, width = left.shape
    for b in range(blocks):
        values, total = block_of(numer, counts, b, q, height)
        high, low = split(total)
        values = close(values, high, low).astype(BF)
        left[b] = values[:, :width]
        right[b] = values[:, width:]


def keep_kernel(place, stats, rows, norms, own, up, down, far, up2, down2, far2, kept, held, numer, counts):
    q = place[1]
    pieces = [(own, lse_of(stats, place[2]))] + half_pieces(place, stats, (up, down, far), 0)
    pieces += half_pieces(place, stats, (up2, down2, far2), 1)
    weighted(pieces, rows, norms, q, held, numer, counts)
    blocks, height, _ = kept.shape
    for b in range(blocks):
        values, total = block_of(numer, counts, b, q, height)
        kept[b] = close(values, total, jnp.zeros_like(total))


def merge_kernel(kept, left, right, send):
    blocks, height, _ = kept.shape
    for b in range(blocks):
        at = 0
        for got in (left, right):
            width = got.shape[2]
            values = kept[b, :, at : at + width] + got[b].astype(F32)
            tail = values[height - 8 :]
            counts = tail[8 - TAIL : 9 - TAIL, :LANES] + tail[9 - TAIL : 10 - TAIL, :LANES]
            high, low = split(counts)
            values = close(values, high, low).astype(BF)
            for c in range(width // LANES):
                send[b * N_CENT + at // LANES + c] = values[:, c * LANES : (c + 1) * LANES]
            at += width


def final_kernel(got, out, scratch):
    n, height, _ = got.shape
    slot = height - TAIL
    for c in range(N_CENT):
        values = got[c].astype(F32)
        for i in range(1, n // N_CENT):
            values += got[i * N_CENT + c].astype(F32)
        tail = values[height - 8 :]
        counts = tail[8 - TAIL : 9 - TAIL] + tail[9 - TAIL : 10 - TAIL] + 1.0
        column = jnp.broadcast_to(counts, (LANES, LANES)).T
        scratch[c * slot : (c + 1) * slot] = (values / column[:height])[:slot]
    out[...] = scratch[...].astype(BF)


def body(points, centroids):
    rows, dim = centroids.shape
    pts = points.shape[0]
    n_blocks = NZ // 2
    slot = rows // (NX * NZ)
    height = slot + TAIL
    half = pts // NC
    x, core, parity = (lax.axis_index(a) for a in ("x", "core", "zp"))
    place = jnp.stack([core, parity, x]).astype(jnp.int32)
    shape = jax.ShapeDtypeStruct

    own_half = pl.pallas_call(
        cut_kernel,
        out_shape=shape((half, dim), BF),
        in_specs=[SMEM, VMEM, ANY],
        out_specs=VMEM,
        compiler_params=params(50),
        cost_estimate=CHEAP,
        name="cut",
    )(place, points, centroids)
    near = [lax.ppermute(own_half, "x", [(i, (i + k) % NX) for i in range(NX)]) for k in SHIFTS]

    stats_shape = (NX * N_CENT, 2 * pts // LANES, LANES)
    send_stats, flag = pl.pallas_call(
        stats_kernel,
        out_shape=(shape(stats_shape, F32), shape((8, LANES), F32)),
        in_specs=[VMEM, VMEM, ANY],
        out_specs=(VMEM, VMEM),
        compiler_params=params(16),
        cost_estimate=CHEAP,
        name="stats",
    )(points, centroids, own_half)
    stats = lax.all_to_all(send_stats, ("x", *CENT), 0, 0)
    work = n_blocks * (-(-(slot + 12) // 16) * 16)
    mine, norms = pl.pallas_call(
        window_kernel,
        out_shape=(shape((2, work, dim), BF), shape((2, work, 1), F32)),
        in_specs=[SMEM, ANY, ANY],
        out_specs=(VMEM, VMEM),
        scratch_shapes=[pltpu.SemaphoreType.DMA((NZ,))],
        compiler_params=params(50),
        cost_estimate=CHEAP,
        name="window",
    )(place, centroids, flag)

    def call(kernel, out_shape, n_points, *args, scratch=()):
        return pl.pallas_call(
            kernel,
            out_shape=out_shape,
            in_specs=[SMEM] + [VMEM] * (3 + len(args)),
            out_specs=jax.tree.map(lambda _: VMEM, out_shape),
            scratch_shapes=[pltpu.VMEM((n_points, dim), BF), *scratch],
            compiler_params=params(28),
            cost_estimate=CHEAP,
            name=kernel.__name__,
        )(place, stats, mine, norms, *args)

    sums = (shape((work, dim), F32), shape((work, LANES), F32))
    spare = [pltpu.VMEM(s.shape, F32) for s in sums]
    near, stats, mine, norms = lax.optimization_barrier((near, stats, mine, norms))
    others = [lax.ppermute(a, "core", [(0, 1), (1, 0)]) for a in near]
    numer = call(first_kernel, sums, pts + 3 * half, points, *near)
    others, numer = lax.optimization_barrier((others, numer))
    parts = tuple(shape((n_blocks, height, width), BF) for width in (LEFT, dim - LEFT))
    left, right = call(give_kernel, parts, 3 * half, *others, *numer, scratch=spare)

    got_left = lax.ppermute(left, Z, [(i, i ^ 1) for i in range(NZ)])
    got_right = lax.ppermute(right, Z, [(i, (i + (1 if i % 2 else -1)) % NZ) for i in range(NZ)])
    kept = call(keep_kernel, shape((n_blocks, height, dim), F32), NX * pts, points, *near, *others, scratch=spare)
    send = pl.pallas_call(
        merge_kernel,
        out_shape=shape((n_blocks * N_CENT, height, LANES), BF),
        in_specs=[VMEM] * 3,
        out_specs=VMEM,
        compiler_params=params(16),
        name="merge",
    )(kept, got_left, got_right)
    got = lax.all_to_all(send, ("zq", *CENT), 0, 0)
    return pl.pallas_call(
        final_kernel,
        out_shape=shape((N_CENT * slot, LANES), BF),
        in_specs=[VMEM],
        out_specs=VMEM,
        scratch_shapes=[pltpu.VMEM((N_CENT * slot, LANES), F32)],
        compiler_params=params(16),
        name="final",
    )(got)


def solution(mesh):
    fine = Mesh(mesh.devices.reshape(NX, NZ // 2, 2, NY, NC), ("x", *Z, *CENT))
    pts = ("x", *Z)
    return jax.shard_map(
        body, mesh=fine, in_specs=(P(pts, None), P(CENT, None)), out_specs=P(pts, CENT), check_vma=False
    )
```

```python
import functools

import jax
import jax.numpy as jnp
from jax import lax
from jax.experimental import pallas as pl
from jax.experimental.pallas import tpu as pltpu
from jax.sharding import Mesh, PartitionSpec as P

BF = jnp.bfloat16
F32 = jnp.float32
NX, NZ, NY, NC = 4, 8, 4, 2
Z = ("zq", "zp")
CENT = ("y", "core")
N_CENT = NY * NC
LANES = 128
TAIL = 4
VMEM = pl.BlockSpec(memory_space=pltpu.VMEM)
SMEM = pl.BlockSpec(memory_space=pltpu.SMEM)
ANY = pl.BlockSpec(memory_space=pl.ANY)
MIB = 2**20
CHEAP = pl.CostEstimate(flops=1, bytes_accessed=1, transcendentals=0)
CHUNKS = 5
LEFT = 640
SHIFTS = (1, NX - 1, 2)


def dot_nt(a, b):
    return lax.dot_general(a, b, (((1,), (1,)), ((), ())), preferred_element_type=F32)


def params(mib):
    return pltpu.CompilerParams(vmem_limit_bytes=mib * MIB)


def cut_kernel(place, points, cents, half_out, held, sems):
    half = held.shape[0]
    here = points.at[pl.ds(pl.multiple_of(place[0] * half, half), half)]
    for i, (source, target) in enumerate(((here, held), (held, half_out))):
        copy = pltpu.make_async_copy(source, target, sems.at[i])
        copy.start()
        copy.wait()


def stats_kernel(points, cents, after, out, flag):
    chunk = cents.shape[0] // CHUNKS
    pts = points[...]
    tops, totals = [], []
    for i in range(CHUNKS):
        rows = cents[i * chunk : (i + 1) * chunk]
        wide = rows.astype(F32)
        logits = dot_nt(rows, pts) - 0.5 * jnp.sum(wide * wide, axis=1, keepdims=True)
        top = jnp.max(logits, axis=0, keepdims=True)
        tops.append(top)
        totals.append(jnp.sum(jnp.exp(logits - top), axis=0, keepdims=True))
    top = functools.reduce(jnp.maximum, tops)
    total = sum(s * jnp.exp(t - top) for s, t in zip(totals, tops))
    groups = top.shape[1] // LANES
    both = [r[:, g * LANES : (g + 1) * LANES] for r in (top, total) for g in range(groups)]
    out[...] = jnp.broadcast_to(jnp.concatenate(both, axis=0)[None], out.shape)
    flag[...] = jnp.zeros_like(flag)


def window_kernel(place, table, after, mine, norms, sems):
    _, work, _ = mine.shape
    count = NZ // 2
    window = work // count
    stride = table.shape[0] // NX
    slot = stride // NZ
    copies = {}
    for q in range(2):
        for i in range(count):
            at = pl.multiple_of(place[2] * stride + (2 * i + q) * slot // 16 * 16, 16)
            to = mine.at[q, pl.ds(i * window, window)]
            copies[q, i] = pltpu.make_async_copy(table.at[pl.ds(at, window)], to, sems.at[q * count + i])
    for copy in copies.values():
        copy.start()
    for (q, i), copy in copies.items():
        copy.wait()
        here = slice(i * window, (i + 1) * window)
        wide = mine[q, here].astype(F32)
        norms[q, here] = 0.5 * jnp.sum(wide * wide, axis=1, keepdims=True)


def lse_of(stats, source):
    groups = stats.shape[1] // 2
    part = stats[pl.ds(source * N_CENT, N_CENT)]
    m, s = part[:, :groups], part[:, groups:]
    high = jnp.max(m, axis=0)
    return high + jnp.log(jnp.sum(s * jnp.exp(m - high[None]), axis=0))


def lse_halves(place, stats, k):
    lse = lse_of(stats, lax.rem(place[2] + NX - k, NX))
    half = lse.shape[0] // 2
    first = place[0] == 0
    return jnp.where(first, lse[:half], lse[half:]), jnp.where(first, lse[half:], lse[:half])


def weighted(pieces, rows, norms, q, held, numer, counts, before=None):
    at = 0
    lse = []
    for ref, part in pieces:
        held[at : at + ref.shape[0]] = ref[...]
        lse += [part[g : g + 1] for g in range(part.shape[0])]
        at += ref.shape[0]
    logits = dot_nt(rows[q], held[...])
    shift = norms[q]
    some = jnp.zeros(counts.shape, F32)
    weights = []
    for g, part in enumerate(lse):
        w = jnp.exp(logits[:, g * LANES : (g + 1) * LANES] - shift - part).astype(BF)
        some += w.astype(F32)
        weights.append(w)
    more = jnp.dot(jnp.concatenate(weights, axis=1), held[...], preferred_element_type=F32)
    if before is not None:
        more, some = before[0][...] + more, before[1][...] + some
    numer[...] = more
    counts[...] = some


def block_of(numer, counts, i, q, height):
    start = i * (numer.shape[0] * 2 // NZ) + 8 * (i % 2)
    found = []
    for ref in (numer, counts):
        v = ref[start : start + height]
        found.append(jnp.where(q == 1, jnp.concatenate([v[4:], v[:4]], axis=0), v))
    return found[0], row_counts(found[1])


def row_counts(part):
    part = jnp.concatenate([part, jnp.zeros((LANES - part.shape[0], LANES), F32)], axis=0)
    return jnp.sum(part.T, axis=0, keepdims=True)


def close(values, first, second):
    height, width = values.shape
    first = jnp.concatenate([first] * (width // LANES), axis=1)
    second = jnp.concatenate([second] * (width // LANES), axis=1)
    last = values[height - 8 :]
    row = lax.broadcasted_iota(jnp.int32, last.shape, 0)
    last = jnp.where(row == 8 - TAIL, first, jnp.where(row == 9 - TAIL, second, jnp.where(row > 9 - TAIL, 0.0, last)))
    return jnp.concatenate([values[: height - 8], last], axis=0)


def split(counts):
    high = counts.astype(BF).astype(F32)
    return high, counts - high


def half_pieces(place, stats, refs, which):
    return [(ref, lse_halves(place, stats, k)[which]) for k, ref in zip(SHIFTS, refs)]


def first_kernel(place, stats, rows, norms, own, up, down, far, numer, counts, held):
    pieces = [(own, lse_of(stats, place[2]))] + half_pieces(place, stats, (up, down, far), 0)
    weighted(pieces, rows, norms, 1 - place[1], held, numer, counts)


def give_kernel(place, stats, rows, norms, up, down, far, numer_in, counts_in, left, right, held, numer, counts):
    q = 1 - place[1]
    pieces = half_pieces(place, stats, (up, down, far), 1)
    weighted(pieces, rows, norms, q, held, numer, counts, (numer_in, counts_in))
    blocks, height, width = left.shape
    for b in range(blocks):
        values, total = block_of(numer, counts, b, q, height)
        high, low = split(total)
        values = close(values, high, low).astype(BF)
        left[b] = values[:, :width]
        right[b] = values[:, width:]


def keep_kernel(place, stats, rows, norms, own, up, down, far, up2, down2, far2, kept, held, numer, counts):
    q = place[1]
    pieces = [(own, lse_of(stats, place[2]))] + half_pieces(place, stats, (up, down, far), 0)
    pieces += half_pieces(place, stats, (up2, down2, far2), 1)
    weighted(pieces, rows, norms, q, held, numer, counts)
    blocks, height, _ = kept.shape
    for b in range(blocks):
        values, total = block_of(numer, counts, b, q, height)
        kept[b] = close(values, total, jnp.zeros_like(total))


def merge_kernel(kept, left, right, send):
    blocks, height, _ = kept.shape
    for b in range(blocks):
        at = 0
        for got in (left, right):
            width = got.shape[2]
            values = kept[b, :, at : at + width] + got[b].astype(F32)
            tail = values[height - 8 :]
            counts = tail[8 - TAIL : 9 - TAIL, :LANES] + tail[9 - TAIL : 10 - TAIL, :LANES]
            high, low = split(counts)
            values = close(values, high, low).astype(BF)
            for c in range(width // LANES):
                send[b * N_CENT + at // LANES + c] = values[:, c * LANES : (c + 1) * LANES]
            at += width


def final_kernel(got, out, scratch):
    n, height, _ = got.shape
    slot = height - TAIL
    for c in range(N_CENT):
        values = got[c].astype(F32)
        for i in range(1, n // N_CENT):
            values += got[i * N_CENT + c].astype(F32)
        tail = values[height - 8 :]
        counts = tail[8 - TAIL : 9 - TAIL] + tail[9 - TAIL : 10 - TAIL] + 1.0
        column = jnp.broadcast_to(counts, (LANES, LANES)).T
        scratch[c * slot : (c + 1) * slot] = (values / column[:height])[:slot]
    out[...] = scratch[...].astype(BF)


def body(points, centroids):
    rows, dim = centroids.shape
    pts = points.shape[0]
    n_blocks = NZ // 2
    slot = rows // (NX * NZ)
    height = slot + TAIL
    half = pts // NC
    x, core, parity = (lax.axis_index(a) for a in ("x", "core", "zp"))
    place = jnp.stack([core, parity, x]).astype(jnp.int32)
    shape = jax.ShapeDtypeStruct

    own_half = pl.pallas_call(
        cut_kernel,
        out_shape=shape((half, dim), BF),
        in_specs=[SMEM, ANY, ANY],
        out_specs=ANY,
        scratch_shapes=[pltpu.VMEM((half, dim), BF), pltpu.SemaphoreType.DMA((2,))],
        compiler_params=params(54),
        cost_estimate=CHEAP,
        name="cut",
    )(place, points, centroids)
    near = [lax.ppermute(own_half, "x", [(i, (i + k) % NX) for i in range(NX)]) for k in SHIFTS]

    stats_shape = (NX * N_CENT, 2 * pts // LANES, LANES)
    send_stats, flag = pl.pallas_call(
        stats_kernel,
        out_shape=(shape(stats_shape, F32), shape((8, LANES), F32)),
        in_specs=[VMEM, VMEM, ANY],
        out_specs=(VMEM, VMEM),
        compiler_params=params(16),
        cost_estimate=CHEAP,
        name="stats",
    )(points, centroids, own_half)
    stats = lax.all_to_all(send_stats, ("x", *CENT), 0, 0)
    work = n_blocks * (-(-(slot + 12) // 16) * 16)
    mine, norms = pl.pallas_call(
        window_kernel,
        out_shape=(shape((2, work, dim), BF), shape((2, work, 1), F32)),
        in_specs=[SMEM, ANY, ANY],
        out_specs=(VMEM, VMEM),
        scratch_shapes=[pltpu.SemaphoreType.DMA((NZ,))],
        compiler_params=params(50),
        cost_estimate=CHEAP,
        name="window",
    )(place, centroids, flag)

    def call(kernel, out_shape, n_points, *args, scratch=()):
        return pl.pallas_call(
            kernel,
            out_shape=out_shape,
            in_specs=[SMEM] + [VMEM] * (3 + len(args)),
            out_specs=jax.tree.map(lambda _: VMEM, out_shape),
            scratch_shapes=[pltpu.VMEM((n_points, dim), BF), *scratch],
            compiler_params=params(28),
            cost_estimate=CHEAP,
            name=kernel.__name__,
        )(place, stats, mine, norms, *args)

    sums = (shape((work, dim), F32), shape((work, LANES), F32))
    spare = [pltpu.VMEM(s.shape, F32) for s in sums]
    near, stats, mine, norms = lax.optimization_barrier((near, stats, mine, norms))
    others = [lax.ppermute(a, "core", [(0, 1), (1, 0)]) for a in near]
    numer = call(first_kernel, sums, pts + 3 * half, points, *near)
    others, numer = lax.optimization_barrier((others, numer))
    parts = tuple(shape((n_blocks, height, width), BF) for width in (LEFT, dim - LEFT))
    left, right = call(give_kernel, parts, 3 * half, *others, *numer, scratch=spare)

    got_left = lax.ppermute(left, Z, [(i, i ^ 1) for i in range(NZ)])
    got_right = lax.ppermute(right, Z, [(i, (i + (1 if i % 2 else -1)) % NZ) for i in range(NZ)])
    kept = call(keep_kernel, shape((n_blocks, height, dim), F32), NX * pts, points, *near, *others, scratch=spare)
    send = pl.pallas_call(
        merge_kernel,
        out_shape=shape((n_blocks * N_CENT, height, LANES), BF),
        in_specs=[VMEM] * 3,
        out_specs=VMEM,
        compiler_params=params(16),
        name="merge",
    )(kept, got_left, got_right)
    got = lax.all_to_all(send, ("zq", *CENT), 0, 0)
    return pl.pallas_call(
        final_kernel,
        out_shape=shape((N_CENT * slot, LANES), BF),
        in_specs=[VMEM],
        out_specs=VMEM,
        scratch_shapes=[pltpu.VMEM((N_CENT * slot, LANES), F32)],
        compiler_params=params(16),
        name="final",
    )(got)


def solution(mesh):
    fine = Mesh(mesh.devices.reshape(NX, NZ // 2, 2, NY, NC), ("x", *Z, *CENT))
    pts = ("x", *Z)
    return jax.shard_map(
        body, mesh=fine, in_specs=(P(pts, None), P(CENT, None)), out_specs=P(pts, CENT), check_vma=False
    )
```

```python
import functools

import jax
import jax.numpy as jnp
from jax import lax
from jax.experimental import pallas as pl
from jax.experimental.pallas import tpu as pltpu
from jax.sharding import Mesh, PartitionSpec as P

BF = jnp.bfloat16
F32 = jnp.float32
NX, NZ, NY, NC = 4, 8, 4, 2
Z = ("zq", "zp")
CENT = ("y", "core")
N_CENT = NY * NC
LANES = 128
TAIL = 4
VMEM = pl.BlockSpec(memory_space=pltpu.VMEM)
SMEM = pl.BlockSpec(memory_space=pltpu.SMEM)
ANY = pl.BlockSpec(memory_space=pl.ANY)
MIB = 2**20
CHEAP = pl.CostEstimate(flops=1, bytes_accessed=1, transcendentals=0)
CHUNKS = 5
LEFT = 640
SHIFTS = (1, NX - 1, 2)


def dot_nt(a, b):
    return lax.dot_general(a, b, (((1,), (1,)), ((), ())), preferred_element_type=F32)


def params(mib):
    return pltpu.CompilerParams(vmem_limit_bytes=mib * MIB)


def cut_kernel(place, points, cents, half_out):
    half = half_out.shape[0]
    half_out[...] = points[pl.ds(pl.multiple_of(place[0] * half, half), half)]


def stats_kernel(points, cents, after, out, flag):
    chunk = cents.shape[0] // CHUNKS
    pts = points[...]
    tops, totals = [], []
    for i in range(CHUNKS):
        rows = cents[i * chunk : (i + 1) * chunk]
        wide = rows.astype(F32)
        logits = dot_nt(rows, pts) - 0.5 * jnp.sum(wide * wide, axis=1, keepdims=True)
        top = jnp.max(logits, axis=0, keepdims=True)
        tops.append(top)
        totals.append(jnp.sum(jnp.exp(logits - top), axis=0, keepdims=True))
    top = functools.reduce(jnp.maximum, tops)
    total = sum(s * jnp.exp(t - top) for s, t in zip(totals, tops))
    groups = top.shape[1] // LANES
    both = [r[:, g * LANES : (g + 1) * LANES] for r in (top, total) for g in range(groups)]
    out[...] = jnp.broadcast_to(jnp.concatenate(both, axis=0)[None], out.shape)
    flag[...] = jnp.zeros_like(flag)


def window_kernel(place, table, after, mine, norms, sems):
    _, work, _ = mine.shape
    count = NZ // 2
    window = work // count
    stride = table.shape[0] // NX
    slot = stride // NZ
    copies = {}
    for q in range(2):
        for i in range(count):
            at = pl.multiple_of(place[2] * stride + (2 * i + q) * slot // 16 * 16, 16)
            to = mine.at[q, pl.ds(i * window, window)]
            copies[q, i] = pltpu.make_async_copy(table.at[pl.ds(at, window)], to, sems.at[q * count + i])
    for copy in copies.values():
        copy.start()
    for (q, i), copy in copies.items():
        copy.wait()
        here = slice(i * window, (i + 1) * window)
        wide = mine[q, here].astype(F32)
        norms[q, here] = 0.5 * jnp.sum(wide * wide, axis=1, keepdims=True)


def lse_of(stats, source):
    groups = stats.shape[1] // 2
    part = stats[pl.ds(source * N_CENT, N_CENT)]
    m, s = part[:, :groups], part[:, groups:]
    high = jnp.max(m, axis=0)
    return high + jnp.log(jnp.sum(s * jnp.exp(m - high[None]), axis=0))


def lse_halves(place, stats, k):
    lse = lse_of(stats, lax.rem(place[2] + NX - k, NX))
    half = lse.shape[0] // 2
    first = place[0] == 0
    return jnp.where(first, lse[:half], lse[half:]), jnp.where(first, lse[half:], lse[:half])


def weighted(pieces, rows, norms, q, held, numer, counts, before=None):
    at = 0
    lse = []
    for ref, part in pieces:
        held[at : at + ref.shape[0]] = ref[...]
        lse += [part[g : g + 1] for g in range(part.shape[0])]
        at += ref.shape[0]
    logits = dot_nt(rows[q], held[...])
    shift = norms[q]
    some = jnp.zeros(counts.shape, F32)
    weights = []
    for g, part in enumerate(lse):
        w = jnp.exp(logits[:, g * LANES : (g + 1) * LANES] - shift - part).astype(BF)
        some += w.astype(F32)
        weights.append(w)
    more = jnp.dot(jnp.concatenate(weights, axis=1), held[...], preferred_element_type=F32)
    if before is not None:
        more, some = before[0][...] + more, before[1][...] + some
    numer[...] = more
    counts[...] = some


def block_of(numer, counts, i, q, height):
    start = i * (numer.shape[0] * 2 // NZ) + 8 * (i % 2)
    found = []
    for ref in (numer, counts):
        v = ref[start : start + height]
        found.append(jnp.where(q == 1, jnp.concatenate([v[4:], v[:4]], axis=0), v))
    return found[0], row_counts(found[1])


def row_counts(part):
    part = jnp.concatenate([part, jnp.zeros((LANES - part.shape[0], LANES), F32)], axis=0)
    return jnp.sum(part.T, axis=0, keepdims=True)


def close(values, first, second):
    height, width = values.shape
    first = jnp.concatenate([first] * (width // LANES), axis=1)
    second = jnp.concatenate([second] * (width // LANES), axis=1)
    last = values[height - 8 :]
    row = lax.broadcasted_iota(jnp.int32, last.shape, 0)
    last = jnp.where(row == 8 - TAIL, first, jnp.where(row == 9 - TAIL, second, jnp.where(row > 9 - TAIL, 0.0, last)))
    return jnp.concatenate([values[: height - 8], last], axis=0)


def split(counts):
    high = counts.astype(BF).astype(F32)
    return high, counts - high


def half_pieces(place, stats, refs, which):
    return [(ref, lse_halves(place, stats, k)[which]) for k, ref in zip(SHIFTS, refs)]


def first_kernel(place, stats, rows, norms, own, up, down, far, numer, counts, held, sems):
    refs = (own, up, down, far)
    parts = [lse_of(stats, place[2])] + [lse_halves(place, stats, k)[0] for k in SHIFTS]
    copies, spans, at = [], [], 0
    for i, ref in enumerate(refs):
        n = ref.shape[0]
        copies.append(pltpu.make_async_copy(ref, held.at[pl.ds(at, n)], sems.at[i]))
        spans.append((at, n))
        at += n
    for copy in copies:
        copy.start()
    q = 1 - place[1]
    mine, shift = rows[q], norms[q]
    some = jnp.zeros(counts.shape, F32)
    weights = []
    for copy, (at, n), part in zip(copies, spans, parts):
        copy.wait()
        logits = dot_nt(mine, held[at : at + n])
        for g in range(n // LANES):
            w = jnp.exp(logits[:, g * LANES : (g + 1) * LANES] - shift - part[g : g + 1]).astype(BF)
            some += w.astype(F32)
            weights.append(w)
    numer[...] = jnp.dot(jnp.concatenate(weights, axis=1), held[...], preferred_element_type=F32)
    counts[...] = some


def give_kernel(place, stats, rows, norms, up, down, far, numer_in, counts_in, left, right, held, numer, counts):
    q = 1 - place[1]
    pieces = half_pieces(place, stats, (up, down, far), 1)
    weighted(pieces, rows, norms, q, held, numer, counts, (numer_in, counts_in))
    blocks, height, width = left.shape
    for b in range(blocks):
        values, total = block_of(numer, counts, b, q, height)
        high, low = split(total)
        values = close(values, high, low).astype(BF)
        left[b] = values[:, :width]
        right[b] = values[:, width:]


def keep_kernel(place, stats, rows, norms, own, up, down, far, up2, down2, far2, kept, held, numer, counts):
    q = place[1]
    pieces = [(own, lse_of(stats, place[2]))] + half_pieces(place, stats, (up, down, far), 0)
    pieces += half_pieces(place, stats, (up2, down2, far2), 1)
    weighted(pieces, rows, norms, q, held, numer, counts)
    blocks, height, _ = kept.shape
    for b in range(blocks):
        values, total = block_of(numer, counts, b, q, height)
        kept[b] = close(values, total, jnp.zeros_like(total))


def merge_kernel(kept, left, right, send):
    blocks, height, _ = kept.shape
    for b in range(blocks):
        at = 0
        for got in (left, right):
            width = got.shape[2]
            values = kept[b, :, at : at + width] + got[b].astype(F32)
            tail = values[height - 8 :]
            counts = tail[8 - TAIL : 9 - TAIL, :LANES] + tail[9 - TAIL : 10 - TAIL, :LANES]
            high, low = split(counts)
            values = close(values, high, low).astype(BF)
            for c in range(width // LANES):
                send[b * N_CENT + at // LANES + c] = values[:, c * LANES : (c + 1) * LANES]
            at += width


def final_kernel(got, out, scratch):
    n, height, _ = got.shape
    slot = height - TAIL
    for c in range(N_CENT):
        values = got[c].astype(F32)
        for i in range(1, n // N_CENT):
            values += got[i * N_CENT + c].astype(F32)
        tail = values[height - 8 :]
        counts = tail[8 - TAIL : 9 - TAIL] + tail[9 - TAIL : 10 - TAIL] + 1.0
        column = jnp.broadcast_to(counts, (LANES, LANES)).T
        scratch[c * slot : (c + 1) * slot] = (values / column[:height])[:slot]
    out[...] = scratch[...].astype(BF)


def body(points, centroids):
    rows, dim = centroids.shape
    pts = points.shape[0]
    n_blocks = NZ // 2
    slot = rows // (NX * NZ)
    height = slot + TAIL
    half = pts // NC
    x, core, parity = (lax.axis_index(a) for a in ("x", "core", "zp"))
    place = jnp.stack([core, parity, x]).astype(jnp.int32)
    shape = jax.ShapeDtypeStruct

    own_half = pl.pallas_call(
        cut_kernel,
        out_shape=shape((half, dim), BF),
        in_specs=[SMEM, VMEM, ANY],
        out_specs=VMEM,
        compiler_params=params(50),
        cost_estimate=CHEAP,
        name="cut",
    )(place, points, centroids)
    near = [lax.ppermute(own_half, "x", [(i, (i + k) % NX) for i in range(NX)]) for k in SHIFTS]

    stats_shape = (NX * N_CENT, 2 * pts // LANES, LANES)
    send_stats, flag = pl.pallas_call(
        stats_kernel,
        out_shape=(shape(stats_shape, F32), shape((8, LANES), F32)),
        in_specs=[VMEM, VMEM, ANY],
        out_specs=(VMEM, VMEM),
        compiler_params=params(16),
        cost_estimate=CHEAP,
        name="stats",
    )(points, centroids, own_half)
    stats = lax.all_to_all(send_stats, ("x", *CENT), 0, 0)
    work = n_blocks * (-(-(slot + 12) // 16) * 16)
    mine, norms = pl.pallas_call(
        window_kernel,
        out_shape=(shape((2, work, dim), BF), shape((2, work, 1), F32)),
        in_specs=[SMEM, ANY, ANY],
        out_specs=(VMEM, VMEM),
        scratch_shapes=[pltpu.SemaphoreType.DMA((NZ,))],
        compiler_params=params(50),
        cost_estimate=CHEAP,
        name="window",
    )(place, centroids, flag)

    def call(kernel, out_shape, n_points, *args, scratch=(), place_of=VMEM):
        return pl.pallas_call(
            kernel,
            out_shape=out_shape,
            in_specs=[SMEM] + [VMEM] * 3 + [place_of] * len(args),
            out_specs=jax.tree.map(lambda _: VMEM, out_shape),
            scratch_shapes=[pltpu.VMEM((n_points, dim), BF), *scratch],
            compiler_params=params(28),
            cost_estimate=CHEAP,
            name=kernel.__name__,
        )(place, stats, mine, norms, *args)

    sums = (shape((work, dim), F32), shape((work, LANES), F32))
    spare = [pltpu.VMEM(s.shape, F32) for s in sums]
    near, stats, mine, norms = lax.optimization_barrier((near, stats, mine, norms))
    others = [lax.ppermute(a, "core", [(0, 1), (1, 0)]) for a in near]
    waits = [pltpu.SemaphoreType.DMA((1 + len(near),))]
    numer = call(first_kernel, sums, pts + 3 * half, points, *near, scratch=waits, place_of=ANY)
    others, numer = lax.optimization_barrier((others, numer))
    parts = tuple(shape((n_blocks, height, width), BF) for width in (LEFT, dim - LEFT))
    left, right = call(give_kernel, parts, 3 * half, *others, *numer, scratch=spare)

    got_left = lax.ppermute(left, Z, [(i, i ^ 1) for i in range(NZ)])
    got_right = lax.ppermute(right, Z, [(i, (i + (1 if i % 2 else -1)) % NZ) for i in range(NZ)])
    kept = call(keep_kernel, shape((n_blocks, height, dim), F32), NX * pts, points, *near, *others, scratch=spare)
    send = pl.pallas_call(
        merge_kernel,
        out_shape=shape((n_blocks * N_CENT, height, LANES), BF),
        in_specs=[VMEM] * 3,
        out_specs=VMEM,
        compiler_params=params(16),
        name="merge",
    )(kept, got_left, got_right)
    got = lax.all_to_all(send, ("zq", *CENT), 0, 0)
    return pl.pallas_call(
        final_kernel,
        out_shape=shape((N_CENT * slot, LANES), BF),
        in_specs=[VMEM],
        out_specs=VMEM,
        scratch_shapes=[pltpu.VMEM((N_CENT * slot, LANES), F32)],
        compiler_params=params(16),
        name="final",
    )(got)


def solution(mesh):
    fine = Mesh(mesh.devices.reshape(NX, NZ // 2, 2, NY, NC), ("x", *Z, *CENT))
    pts = ("x", *Z)
    return jax.shard_map(
        body, mesh=fine, in_specs=(P(pts, None), P(CENT, None)), out_specs=P(pts, CENT), check_vma=False
    )
```

```python
import functools

import jax
import jax.numpy as jnp
from jax import lax
from jax.experimental import pallas as pl
from jax.experimental.pallas import tpu as pltpu
from jax.sharding import Mesh, PartitionSpec as P

BF = jnp.bfloat16
F32 = jnp.float32
NX, NZ, NY, NC = 4, 8, 4, 2
Z = ("zq", "zp")
CENT = ("y", "core")
N_CENT = NY * NC
LANES = 128
TAIL = 4
VMEM = pl.BlockSpec(memory_space=pltpu.VMEM)
SMEM = pl.BlockSpec(memory_space=pltpu.SMEM)
ANY = pl.BlockSpec(memory_space=pl.ANY)
MIB = 2**20
CHEAP = pl.CostEstimate(flops=1, bytes_accessed=1, transcendentals=0)
CHUNKS = 5
LEFT = 640
SHIFTS = (1, NX - 1, 2)


def dot_nt(a, b):
    return lax.dot_general(a, b, (((1,), (1,)), ((), ())), preferred_element_type=F32)


def params(mib):
    return pltpu.CompilerParams(vmem_limit_bytes=mib * MIB)


def cut_kernel(place, points, cents, half_out):
    half = half_out.shape[0]
    half_out[...] = points[pl.ds(pl.multiple_of(place[0] * half, half), half)]


def stats_kernel(points, cents, after, out, flag):
    chunk = cents.shape[0] // CHUNKS
    pts = points[...]
    tops, totals = [], []
    for i in range(CHUNKS):
        rows = cents[i * chunk : (i + 1) * chunk]
        wide = rows.astype(F32)
        logits = dot_nt(rows, pts) - 0.5 * jnp.sum(wide * wide, axis=1, keepdims=True)
        top = jnp.max(logits, axis=0, keepdims=True)
        tops.append(top)
        totals.append(jnp.sum(jnp.exp(logits - top), axis=0, keepdims=True))
    top = functools.reduce(jnp.maximum, tops)
    total = sum(s * jnp.exp(t - top) for s, t in zip(totals, tops))
    groups = top.shape[1] // LANES
    both = [r[:, g * LANES : (g + 1) * LANES] for r in (top, total) for g in range(groups)]
    out[...] = jnp.broadcast_to(jnp.concatenate(both, axis=0)[None], out.shape)
    flag[...] = jnp.zeros_like(flag)


def window_kernel(place, table, after, mine, norms, sems):
    _, work, _ = mine.shape
    count = NZ // 2
    window = work // count
    stride = table.shape[0] // NX
    slot = stride // NZ
    copies = {}
    for q in range(2):
        for i in range(count):
            at = pl.multiple_of(place[2] * stride + (2 * i + q) * slot // 16 * 16, 16)
            to = mine.at[q, pl.ds(i * window, window)]
            copies[q, i] = pltpu.make_async_copy(table.at[pl.ds(at, window)], to, sems.at[q * count + i])
    for copy in copies.values():
        copy.start()
    for (q, i), copy in copies.items():
        copy.wait()
        here = slice(i * window, (i + 1) * window)
        wide = mine[q, here].astype(F32)
        norms[q, here] = 0.5 * jnp.sum(wide * wide, axis=1, keepdims=True)


def lse_of(stats, source):
    groups = stats.shape[1] // 2
    part = stats[pl.ds(source * N_CENT, N_CENT)]
    m, s = part[:, :groups], part[:, groups:]
    high = jnp.max(m, axis=0)
    return high + jnp.log(jnp.sum(s * jnp.exp(m - high[None]), axis=0))


def lse_halves(place, stats, k):
    lse = lse_of(stats, lax.rem(place[2] + NX - k, NX))
    half = lse.shape[0] // 2
    first = place[0] == 0
    return jnp.where(first, lse[:half], lse[half:]), jnp.where(first, lse[half:], lse[:half])


def weighted(pieces, rows, norms, q, held, numer, counts, before=None):
    at = 0
    lse = []
    for ref, part in pieces:
        held[at : at + ref.shape[0]] = ref[...]
        lse += [part[g : g + 1] for g in range(part.shape[0])]
        at += ref.shape[0]
    logits = dot_nt(rows[q], held[...])
    shift = norms[q]
    some = jnp.zeros(counts.shape, F32)
    weights = []
    for g, part in enumerate(lse):
        w = jnp.exp(logits[:, g * LANES : (g + 1) * LANES] - shift - part).astype(BF)
        some += w.astype(F32)
        weights.append(w)
    more = jnp.dot(jnp.concatenate(weights, axis=1), held[...], preferred_element_type=F32)
    if before is not None:
        more, some = before[0][...] + more, before[1][...] + some
    numer[...] = more
    counts[...] = some


def block_of(numer, counts, i, q, height):
    start = i * (numer.shape[0] * 2 // NZ) + 8 * (i % 2)
    found = []
    for ref in (numer, counts):
        v = ref[start : start + height]
        found.append(jnp.where(q == 1, jnp.concatenate([v[4:], v[:4]], axis=0), v))
    return found[0], row_counts(found[1])


def row_counts(part):
    part = jnp.concatenate([part, jnp.zeros((LANES - part.shape[0], LANES), F32)], axis=0)
    return jnp.sum(part.T, axis=0, keepdims=True)


def close(values, first, second):
    height, width = values.shape
    first = jnp.concatenate([first] * (width // LANES), axis=1)
    second = jnp.concatenate([second] * (width // LANES), axis=1)
    last = values[height - 8 :]
    row = lax.broadcasted_iota(jnp.int32, last.shape, 0)
    last = jnp.where(row == 8 - TAIL, first, jnp.where(row == 9 - TAIL, second, jnp.where(row > 9 - TAIL, 0.0, last)))
    return jnp.concatenate([values[: height - 8], last], axis=0)


def split(counts):
    high = counts.astype(BF).astype(F32)
    return high, counts - high


def half_pieces(place, stats, refs, which):
    return [(ref, lse_halves(place, stats, k)[which]) for k, ref in zip(SHIFTS, refs)]


def first_kernel(place, stats, rows, norms, own, up, down, far, numer, counts, held):
    pieces = [(own, lse_of(stats, place[2]))] + half_pieces(place, stats, (up, down, far), 0)
    weighted(pieces, rows, norms, 1 - place[1], held, numer, counts)


def give_kernel(place, stats, rows, norms, up, down, far, numer_in, counts_in, left, right, held, numer, counts):
    q = 1 - place[1]
    pieces = half_pieces(place, stats, (up, down, far), 1)
    weighted(pieces, rows, norms, q, held, numer, counts, (numer_in, counts_in))
    blocks, height, width = left.shape
    for b in range(blocks):
        values, total = block_of(numer, counts, b, q, height)
        high, low = split(total)
        values = close(values, high, low).astype(BF)
        left[b] = values[:, :width]
        right[b] = values[:, width:]


def keep_kernel(place, stats, rows, norms, own, up, down, far, up2, down2, far2, kept, held, numer, counts):
    q = place[1]
    pieces = [(own, lse_of(stats, place[2]))] + half_pieces(place, stats, (up, down, far), 0)
    pieces += half_pieces(place, stats, (up2, down2, far2), 1)
    weighted(pieces, rows, norms, q, held, numer, counts)
    blocks, height, _ = kept.shape
    for b in range(blocks):
        values, total = block_of(numer, counts, b, q, height)
        kept[b] = close(values, total, jnp.zeros_like(total))


def merge_kernel(kept, left, right, send):
    blocks, height, _ = kept.shape
    for b in range(blocks):
        at = 0
        for got in (left, right):
            width = got.shape[2]
            values = kept[b, :, at : at + width] + got[b].astype(F32)
            tail = values[height - 8 :]
            counts = tail[8 - TAIL : 9 - TAIL, :LANES] + tail[9 - TAIL : 10 - TAIL, :LANES]
            high, low = split(counts)
            values = close(values, high, low).astype(BF)
            for c in range(width // LANES):
                send[b * N_CENT + at // LANES + c] = values[:, c * LANES : (c + 1) * LANES]
            at += width


def final_kernel(got, out, scratch):
    n, height, _ = got.shape
    slot = height - TAIL
    for c in range(N_CENT):
        values = got[c].astype(F32)
        for i in range(1, n // N_CENT):
            values += got[i * N_CENT + c].astype(F32)
        tail = values[height - 8 :]
        counts = tail[8 - TAIL : 9 - TAIL] + tail[9 - TAIL : 10 - TAIL] + 1.0
        column = jnp.broadcast_to(counts, (LANES, LANES)).T
        scratch[c * slot : (c + 1) * slot] = (values / column[:height])[:slot]
    out[...] = scratch[...].astype(BF)


def body(points, centroids):
    rows, dim = centroids.shape
    pts = points.shape[0]
    n_blocks = NZ // 2
    slot = rows // (NX * NZ)
    height = slot + TAIL
    half = pts // NC
    x, core, parity = (lax.axis_index(a) for a in ("x", "core", "zp"))
    place = jnp.stack([core, parity, x]).astype(jnp.int32)
    shape = jax.ShapeDtypeStruct

    own_half = pl.pallas_call(
        cut_kernel,
        out_shape=shape((half, dim), BF),
        in_specs=[SMEM, VMEM, ANY],
        out_specs=VMEM,
        compiler_params=params(50),
        cost_estimate=CHEAP,
        name="cut",
    )(place, points, centroids)
    near = [lax.ppermute(own_half, "x", [(i, (i + k) % NX) for i in range(NX)]) for k in SHIFTS]

    stats_shape = (NX * N_CENT, 2 * pts // LANES, LANES)
    send_stats, flag = pl.pallas_call(
        stats_kernel,
        out_shape=(shape(stats_shape, F32), shape((8, LANES), F32)),
        in_specs=[VMEM, VMEM, ANY],
        out_specs=(VMEM, VMEM),
        compiler_params=params(16),
        cost_estimate=CHEAP,
        name="stats",
    )(points, centroids, own_half)
    stats = lax.all_to_all(send_stats, ("x", *CENT), 0, 0)
    work = n_blocks * (-(-(slot + 12) // 16) * 16)
    mine, norms = pl.pallas_call(
        window_kernel,
        out_shape=(shape((2, work, dim), BF), shape((2, work, 1), F32)),
        in_specs=[SMEM, ANY, ANY],
        out_specs=(VMEM, VMEM),
        scratch_shapes=[pltpu.SemaphoreType.DMA((NZ,))],
        compiler_params=params(50),
        cost_estimate=CHEAP,
        name="window",
    )(place, centroids, flag)

    def call(kernel, out_shape, n_points, *args, scratch=()):
        return pl.pallas_call(
            kernel,
            out_shape=out_shape,
            in_specs=[SMEM] + [VMEM] * (3 + len(args)),
            out_specs=jax.tree.map(lambda _: VMEM, out_shape),
            scratch_shapes=[pltpu.VMEM((n_points, dim), BF), *scratch],
            compiler_params=params(28),
            cost_estimate=CHEAP,
            name=kernel.__name__,
        )(place, stats, mine, norms, *args)

    sums = (shape((work, dim), F32), shape((work, LANES), F32))
    spare = [pltpu.VMEM(s.shape, F32) for s in sums]
    near, stats, mine, norms = lax.optimization_barrier((near, stats, mine, norms))
    others = [lax.ppermute(a, "core", [(0, 1), (1, 0)]) for a in near]
    numer = call(first_kernel, sums, pts + 3 * half, points, *near)
    others, numer = lax.optimization_barrier((others, numer))
    parts = tuple(shape((n_blocks, height, width), BF) for width in (LEFT, dim - LEFT))
    left, right = call(give_kernel, parts, 3 * half, *others, *numer, scratch=spare)

    got_left = lax.ppermute(left, Z, [(i, (i + (1 if i % 2 else -1)) % NZ) for i in range(NZ)])
    got_right = lax.ppermute(right, Z, [(i, i ^ 1) for i in range(NZ)])
    kept = call(keep_kernel, shape((n_blocks, height, dim), F32), NX * pts, points, *near, *others, scratch=spare)
    send = pl.pallas_call(
        merge_kernel,
        out_shape=shape((n_blocks * N_CENT, height, LANES), BF),
        in_specs=[VMEM] * 3,
        out_specs=VMEM,
        compiler_params=params(16),
        name="merge",
    )(kept, got_left, got_right)
    got = lax.all_to_all(send, ("zq", *CENT), 0, 0)
    return pl.pallas_call(
        final_kernel,
        out_shape=shape((N_CENT * slot, LANES), BF),
        in_specs=[VMEM],
        out_specs=VMEM,
        scratch_shapes=[pltpu.VMEM((N_CENT * slot, LANES), F32)],
        compiler_params=params(16),
        name="final",
    )(got)


def solution(mesh):
    fine = Mesh(mesh.devices.reshape(NX, NZ // 2, 2, NY, NC), ("x", *Z, *CENT))
    pts = ("x", *Z)
    return jax.shard_map(
        body, mesh=fine, in_specs=(P(pts, None), P(CENT, None)), out_specs=P(pts, CENT), check_vma=False
    )
```
